1024 devices in a mesh: leaf: 4 (over x), row: 8 (over y, core), col: 32 (over z).
Axes of the slice: x: 4, y: 4, z: 32, core: 2. Of those that a mesh axis runs over, the one named last changes fastest.
Arguments:
- child_inv: bfloat16 [4, 4096, 4096], P('leaf', 'col', 'row'), as said below
- child_panel: bfloat16 [4, 2048, 4096], P('leaf', 'row', 'col'), may hold values from -0.09375 to 0.09375
- child_rhs: bfloat16 [4, 4096, 512], P('leaf', 'row'), may hold values from -6 to 6
- anc_tiles: int32 [4, 16], P('leaf', 'row'), may hold values from 0 to 63, as said below
- root_inv: bfloat16 [8192, 8192], P('col', 'row'), as said below
- root_rhs: bfloat16 [8192, 512], P('row'), may hold values from -6 to 6
Outputs:
- child_sol: bfloat16 [4, 4096, 512], P('leaf', ('row', 'col'))
- root_sol: bfloat16 [8192, 512], P(('row', 'col'))
The draws below stay inside these ranges and needn't reach their ends.
Inputs may be any that keep to these rules, and one draw needn't show every extreme that they name: anc_tiles[k, j] names the root tile that update tile j of child k belongs to; it lies in block row j // 2 of the root, that is among the root tiles (j // 2) * 8 to (j // 2) * 8 + 7, and the entries of one child are distinct. child_inv[k] is lower triangular with a diagonal between 0.5 and 1.5. root_inv is lower triangular with a diagonal between 0.5 and 1.5.
All inputs are finite; a program needn't handle non-finite values.
Results may differ from the reference program's by a relative error of at most 0.035.
Values may be sent and summed in bfloat16 or wider, within the bound.
No kernel may reach another device: no remote copies, remote signals or barrier semaphores. Data moves between devices by JAX's collectives and lax.ppermute only.
A program may use at most 32 MiB of HBM per device.

```python
import jax
import jax.numpy as jnp
from jax import lax

NRHS = 512
TILE = 128
RB = 8
UB = 2
LEAVES = 4
SC = 4096
SR = 8192
UR = 2048
UT = 16
RT = 64
N_ROW = 8


def lower_part(noise, diagonal, order):
    rows_index = lax.broadcasted_iota(jnp.int32, (order, order), 0)
    cols_index = lax.broadcasted_iota(jnp.int32, (order, order), 1)
    strict = jnp.where(rows_index > cols_index, noise, 0.0)
    on_diag = jnp.where(rows_index == cols_index, 1.0, 0.0) * diagonal[..., :, None]
    return strict + on_diag


def draw_child_inv(key, part):
    key = jax.random.fold_in(key, 11)
    noise_key, diag_key = jax.random.split(key)
    shape = (LEAVES, SC, SC)
    noise = jax.random.normal(noise_key, shape, jnp.float32) * SC ** (-0.5)
    diagonal = jax.random.uniform(diag_key, (LEAVES, SC), jnp.float32, 0.5, 1.5)
    return lower_part(noise, diagonal, SC).astype(jnp.bfloat16)


def draw_root_inv(key, part):
    key = jax.random.fold_in(key, 17)
    noise_key, diag_key = jax.random.split(key)
    shape = (SR, SR)
    noise = jax.random.normal(noise_key, shape, jnp.float32) * SR ** (-0.5)
    diagonal = jax.random.uniform(diag_key, (SR,), jnp.float32, 0.5, 1.5)
    return lower_part(noise, diagonal, SR).astype(jnp.bfloat16)


def draw_anc_tiles(key, part):
    key = jax.random.fold_in(key, 23)
    block_rows = UT // UB
    shape = (LEAVES, block_rows, RB)
    scores = jax.random.randint(key, shape, 0, 1 << 20) * RB + jnp.arange(RB, dtype=jnp.int32)
    leaf_index = lax.broadcasted_iota(jnp.int32, shape, 0)
    block_index = lax.broadcasted_iota(jnp.int32, shape, 1)
    tile_index = lax.broadcasted_iota(jnp.int32, shape, 2)
    first_end = (leaf_index == 0) & (block_index == 0) & (tile_index == 0)
    last_end = (leaf_index == 0) & (block_index == block_rows - 1) & (tile_index == RB - 1)
    scores = jnp.where(first_end | last_end, -1, scores)
    ranking = jnp.argsort(scores, axis=-1)
    chosen = ranking[:, :, :UB] + (jnp.arange(block_rows, dtype=jnp.int32) * RB)[None, :, None]
    return chosen.reshape(LEAVES, UT).astype(jnp.int32)


def steps_of(stream_key, extent, cuts, low, high):
    def one(axis_at, shards_of):
        steps = jax.random.uniform(jax.random.fold_in(jax.random.fold_in(stream_key, 6), axis_at), (shards_of,), jnp.float32, low / len(cuts), high / len(cuts))
        return jnp.repeat(jnp.exp(steps), extent[axis_at] // shards_of).reshape((-1,) + (1,) * (len(extent) - axis_at - 1))

    gain = one(*cuts[0])
    for cut in cuts[1:]:
        gain = gain * one(*cut)
    return gain


def centred(key, dims, width, limit, cuts=(), kind=jnp.bfloat16):
    values = jax.random.normal(key, dims, jnp.float32) * width
    if len(cuts) > 0:
        values = steps_of(key, dims, cuts, -0.22, 0.18) * values
    return jnp.clip(values, min=-limit, max=limit).astype(kind)


def setup_inputs(seed: int = 0) -> dict:
    splits = jax.random.split(jax.random.key(seed), 7)
    return {
        "child_inv": draw_child_inv(jax.random.fold_in(splits[6], 71), 0),
        "child_panel": centred(splits[1], (LEAVES, UR, SC), SC ** -0.5, 0.09375, ((0, 4), (1, 8), (2, 32))),
        "child_rhs": centred(splits[2], (LEAVES, SC, NRHS), 1.0, 6.0, ((0, 4), (1, 8))),
        "anc_tiles": draw_anc_tiles(jax.random.fold_in(splits[6], 71), 0),
        "root_inv": draw_root_inv(jax.random.fold_in(splits[6], 71), 0),
        "root_rhs": centred(splits[5], (SR, NRHS), 1.0, 6.0, ((0, 8),)),
    }


def rounded_blocks(matrix, vector, pieces):
    block_width = matrix.shape[1] // pieces
    running = jnp.zeros((matrix.shape[0], vector.shape[1]), jnp.float32)
    for b in range(pieces):
        product = jnp.dot(matrix[:, b * block_width:(b + 1) * block_width],
                          vector[b * block_width:(b + 1) * block_width],
                          preferred_element_type=jnp.float32)
        product = lax.optimization_barrier(product.astype(jnp.bfloat16))
        running = running + product.astype(jnp.float32)
    return running


def reference(child_inv, child_panel, child_rhs, anc_tiles, root_inv, root_rhs):
    forward = []
    landed = jnp.zeros((RT, TILE, NRHS), jnp.float32)
    for k in range(LEAVES):
        solved = rounded_blocks(child_inv[k], child_rhs[k], N_ROW).astype(jnp.bfloat16)
        forward.append(solved)
        update = jnp.dot(child_panel[k], solved, preferred_element_type=jnp.float32)
        landed = landed.at[anc_tiles[k].astype(jnp.int32)].add(update.reshape(UT, TILE, NRHS))
    root_side = (root_rhs.astype(jnp.float32) - landed.reshape(SR, NRHS)).astype(jnp.bfloat16)
    root_forward = rounded_blocks(root_inv, root_side, N_ROW).astype(jnp.bfloat16)
    root_sol = jnp.dot(root_inv.T, root_forward, preferred_element_type=jnp.float32).astype(jnp.bfloat16)
    root_tiles = root_sol.reshape(RT, TILE, NRHS)
    solutions = []
    for k in range(LEAVES):
        gathered = root_tiles[anc_tiles[k].astype(jnp.int32)].reshape(UR, NRHS)
        correction = rounded_blocks(child_panel[k].T, gathered, N_ROW).astype(jnp.bfloat16)
        residue = (forward[k].astype(jnp.float32) - correction.astype(jnp.float32)).astype(jnp.bfloat16)
        solutions.append(jnp.dot(child_inv[k].T, residue, preferred_element_type=jnp.float32).astype(jnp.bfloat16))
    return jnp.stack(solutions), root_sol
```

```python
import jax
import jax.numpy as jnp
from jax import lax
from jax.experimental import pallas as pl
from jax.experimental.pallas import tpu as pltpu
from jax.sharding import Mesh, PartitionSpec as P

BF = jnp.bfloat16
F32 = jnp.float32
TILE = 128
LEAF, Y, CORE, ZHI, ZLO = 4, 4, 2, 8, 4
Z = ("zhi", "zlo")


def exchange(x, axis):
    return lax.all_to_all(x, axis, 0, 0, tiled=True)


def share(x, axis, n):
    return exchange(jnp.broadcast_to(x[None], (n,) + x.shape), axis)


def total(parts):
    return jnp.sum(parts.astype(F32), axis=0)


def dot(a, b, contract):
    return lax.dot_general(a, b, (contract, ((), ())), preferred_element_type=F32)


def place_kernel(slot_ref, upd_ref, rhs_own, rhs_oth, root_own, root_oth, out_ref, side_ref):
    half = rhs_own.shape[1]
    side_ref[:, :half] = rhs_own[...].astype(F32)
    side_ref[:, half:] = rhs_oth[...].astype(F32)
    width = side_ref.shape[0]
    for k in range(LEAF):
        for u in range(4):
            at = pl.ds(pl.multiple_of(slot_ref[k * 4 + u] * TILE, TILE), TILE)
            side_ref[:, at] = side_ref[:, at] - upd_ref[k, :width, u * TILE:(u + 1) * TILE].astype(F32)
    out = dot(side_ref[:, :half].astype(BF), root_own[...], ((1,), (1,)))
    out = out + dot(side_ref[:, half:].astype(BF), root_oth[...], ((1,), (1,)))
    out_ref[...] = out.astype(BF)


def pick_kernel(slot_ref, parts_ref, sol_ref, pick_ref, sum_ref):
    acc = parts_ref[0].astype(F32)
    for k in range(1, LEAF):
        acc = acc + parts_ref[k].astype(F32)
    sum_ref[...] = acc
    sol_ref[...] = acc.astype(BF)
    for u in range(4):
        at = pl.ds(pl.multiple_of(slot_ref[u] * TILE, TILE), TILE)
        pick_ref[:, u * TILE:(u + 1) * TILE] = sum_ref[:, at].astype(BF)


def call(kernel, out_shape, scratch, n_in):
    return pl.pallas_call(
        kernel,
        out_shape=out_shape,
        in_specs=[pl.BlockSpec(memory_space=pltpu.SMEM)]
        + [pl.BlockSpec(memory_space=pltpu.VMEM)] * n_in,
        out_specs=jax.tree.map(lambda _: pl.BlockSpec(memory_space=pltpu.VMEM), out_shape),
        scratch_shapes=scratch,
        compiler_params=pltpu.CompilerParams(vmem_limit_bytes=32 * 1024 * 1024),
    )


def body(child_inv, child_panel, child_rhs, anc_tiles, root_inv, root_rhs):
    inv, panel, rhs, anc = child_inv[0], child_panel[0], child_rhs[0], anc_tiles[0]
    y, core, zlo = lax.axis_index("y"), lax.axis_index("core"), lax.axis_index("zlo")
    rows = root_rhs.shape[0]
    width = rhs.shape[1] // (CORE * ZLO)

    swap = [(s * ZLO + t, t * ZLO + s) for s in range(LEAF) for t in range(ZLO)]
    root_own = lax.ppermute(root_inv, ("leaf", "zlo"), swap)
    n = inv.shape[0]
    packed = jnp.concatenate([inv[:, i:i + n] for i in range(0, inv.shape[1], n)] + [panel], axis=0)
    packed = lax.all_gather(packed, ("core", "zlo"), axis=0, tiled=False)

    part = dot(rhs, inv, ((0,), (1,))).astype(BF)
    part = total(exchange(part.reshape(CORE, -1, part.shape[1]), "core")).astype(BF)
    forward = total(share(part, "y", Y)).astype(BF)

    panel_y = lax.all_gather(panel, "core", axis=0, tiled=True)
    anc_y = lax.all_gather(anc, "core", axis=0, tiled=True)

    chunk = lax.dynamic_slice_in_dim(
        root_rhs.reshape(rows, CORE, ZLO, width), zlo, 1, axis=2
    )[:, :, 0]
    chunk = jnp.transpose(chunk, (1, 2, 0))
    side_own = lax.dynamic_index_in_dim(chunk, core, 0, keepdims=False)
    side_oth = lax.ppermute(
        lax.dynamic_index_in_dim(chunk, 1 - core, 0, keepdims=False), "core", [(0, 1), (1, 0)]
    )

    update = dot(forward, panel_y, ((1,), (1,))).astype(BF)
    both = jnp.concatenate([update, forward], axis=1).reshape(ZLO, width, -1)
    both = exchange(both, "zlo")
    forward_all = jnp.transpose(both[:, :, update.shape[1]:], (1, 0, 2)).reshape(width, -1)
    update = total(both[:, :, :update.shape[1]]).astype(BF)
    root_own, side_oth, update = lax.optimization_barrier((root_own, side_oth, update))
    update = total(exchange(update.reshape(ZHI, width // ZHI, -1), "zhi")).astype(BF)
    root_oth = lax.ppermute(root_own, "core", [(0, 1), (1, 0)])
    update = share(update, "zhi", ZHI).reshape(width, -1)
    names = jnp.zeros((8, update.shape[1]), BF).at[:, :4].set(anc_y.astype(BF)[None])
    root_oth, update = lax.optimization_barrier((root_oth, update))
    update = share(jnp.concatenate([update, names], axis=0), "leaf", LEAF)
    slots = update[:, width, :4].reshape(-1).astype(jnp.int32)

    def local(t):
        return lax.rem(t - y * 16 + core * 8, 16)

    root_part = call(
        place_kernel,
        jax.ShapeDtypeStruct((width, root_inv.shape[0]), BF),
        [pltpu.VMEM((width, 2 * rows), F32)],
        5,
    )(local(slots), update, side_own, side_oth, root_own, root_oth)
    packed, root_part = lax.optimization_barrier((packed, root_part))
    inv_all = packed[:, :inv.size // n].reshape(CORE, ZLO, -1, n, n)
    inv_all = jnp.transpose(inv_all, (0, 1, 3, 2, 4))
    panel_all = packed[:, inv.size // n:].reshape(CORE, ZLO, -1, n)
    panel_all = jnp.transpose(panel_all, (1, 0, 2, 3)).reshape(ZLO, -1, n)
    root_forward = total(share(root_part, "y", Y)).astype(BF)
    sol = jnp.concatenate(
        [dot(root_forward, root_own, ((1,), (0,))), dot(root_forward, root_oth, ((1,), (0,)))], axis=1
    ).astype(BF)
    sol = total(exchange(sol.reshape(ZHI, width // ZHI, -1), "zhi")).astype(BF)
    sol = share(sol, "leaf", LEAF)
    root_sol, picked = call(
        pick_kernel,
        (
            jax.ShapeDtypeStruct((width // ZHI, 2 * rows), BF),
            jax.ShapeDtypeStruct((width // ZHI, 4 * TILE), BF),
        ),
        [pltpu.VMEM((width // ZHI, 2 * rows), F32)],
        1,
    )(local(anc_y), sol)
    picked = share(picked, "zhi", ZHI).reshape(width, -1)

    correction = jnp.concatenate(
        [dot(picked, panel_all[z], ((1,), (0,))) for z in range(ZLO)], axis=1
    ).astype(BF)
    correction = total(share(correction, "y", Y)).astype(BF)
    residue = (forward_all.astype(F32) - correction.astype(F32)).astype(BF)
    inv_all = inv_all.reshape(CORE, -1, inv.shape[1])
    child = jnp.stack([dot(inv_all[c], residue, ((0,), (1,))) for c in range(CORE)]).astype(BF)

    cols = ZHI * ZLO
    child = jnp.transpose(child.reshape(CORE, cols, -1, width), (1, 0, 2, 3)).reshape(cols, -1)
    n_child = child.shape[1]
    own, oth = root_sol[:, :rows], root_sol[:, rows:]
    root = jnp.stack([jnp.where(core == 0, own, oth), jnp.where(core == 0, oth, own)])
    few = width // ZHI
    root = jnp.transpose(root.reshape(CORE, few, cols, -1), (2, 0, 1, 3)).reshape(cols, -1)
    out = exchange(jnp.concatenate([child, root], axis=1).reshape(cols, -1, TILE), Z)
    out = out.reshape(ZHI, ZLO, -1)
    child = total(out[:, :, :n_child]).astype(BF)
    child = jnp.transpose(child.reshape(ZLO, CORE, -1), (1, 0, 2)).reshape(CORE, -1)
    n_child = child.shape[1]
    root = out[:, :, CORE * n_child // ZLO:]
    root = jnp.transpose(root.reshape(ZHI, ZLO, CORE, -1), (2, 1, 0, 3)).reshape(CORE, -1)
    out = exchange(jnp.concatenate([child, root], axis=1).reshape(CORE, -1, TILE), "core")
    out = out.reshape(CORE, -1)
    child = out[:, :n_child].reshape(CORE, ZLO, -1, width)
    child = jnp.transpose(child, (2, 0, 1, 3)).reshape(child.shape[2], -1)
    root = out[:, n_child:].reshape(CORE * ZLO * ZHI * few, -1)
    return child[None], jnp.transpose(root)


def solution(mesh):
    split = Mesh(
        mesh.devices.reshape(LEAF, Y, CORE, ZHI, ZLO), ("leaf", "y", "core", "zhi", "zlo")
    )
    row, col = ("y", "core"), ("zhi", "zlo")
    in_specs = (
        P("leaf", col, row),
        P("leaf", row, col),
        P("leaf", row, None),
        P("leaf", row),
        P(col, row),
        P(row, None),
    )
    out_specs = (P("leaf", row + col, None), P(row + col, None))
    return jax.shard_map(body, mesh=split, in_specs=in_specs, out_specs=out_specs, check_vma=False)
```

```python
import jax
import jax.numpy as jnp
from jax import lax
from jax.experimental import pallas as pl
from jax.experimental.pallas import tpu as pltpu
from jax.sharding import Mesh, PartitionSpec as P

BF = jnp.bfloat16
F32 = jnp.float32
TILE = 128
LEAF, Y, CORE, ZHI, ZLO = 4, 4, 2, 4, 8
Z = ("zhi", "zlo")


def exchange(x, axis):
    return lax.all_to_all(x, axis, 0, 0, tiled=True)


def share(x, axis, n):
    return exchange(jnp.broadcast_to(x[None], (n,) + x.shape), axis)


def total(parts):
    return jnp.sum(parts.astype(F32), axis=0)


def dot(a, b, contract):
    return lax.dot_general(a, b, (contract, ((), ())), preferred_element_type=F32)


def place_kernel(slot_ref, upd_ref, rhs_own, rhs_oth, root_own, root_oth, out_ref, side_ref):
    half = rhs_own.shape[1]
    side_ref[:, :half] = rhs_own[...].astype(F32)
    side_ref[:, half:] = rhs_oth[...].astype(F32)
    width = side_ref.shape[0]
    for k in range(LEAF):
        for u in range(4):
            at = pl.ds(pl.multiple_of(slot_ref[k * 4 + u] * TILE, TILE), TILE)
            side_ref[:, at] = side_ref[:, at] - upd_ref[k, :width, u * TILE:(u + 1) * TILE].astype(F32)
    out = dot(side_ref[:, :half].astype(BF), root_own[...], ((1,), (1,)))
    out = out + dot(side_ref[:, half:].astype(BF), root_oth[...], ((1,), (1,)))
    out_ref[...] = out.astype(BF)


def spread_kernel(slot_ref, parts_ref, root_own, root_oth, out_ref, sol_ref):
    half = root_own.shape[1]
    forward = parts_ref[0].astype(F32)
    for k in range(1, Y):
        forward = forward + parts_ref[k].astype(F32)
    forward = forward.astype(BF)
    sol_ref[:, :half] = dot(forward, root_own[...], ((1,), (0,)))
    sol_ref[:, half:] = dot(forward, root_oth[...], ((1,), (0,)))
    width, span = forward.shape[0], 4 * TILE
    few = width // LEAF
    for k in range(LEAF):
        for u in range(4):
            at = pl.ds(pl.multiple_of(slot_ref[k * 4 + u] * TILE, TILE), TILE)
            out_ref[k, :width, u * TILE:(u + 1) * TILE] = sol_ref[:, at].astype(BF)
        mine = sol_ref[k * few:(k + 1) * few, :]
        mine = jnp.concatenate([mine[:, j * span:(j + 1) * span] for j in range(4)], axis=0)
        out_ref[k, width:, :] = mine.astype(BF)


def call(kernel, out_shape, scratch, n_in):
    return pl.pallas_call(
        kernel,
        out_shape=out_shape,
        in_specs=[pl.BlockSpec(memory_space=pltpu.SMEM)]
        + [pl.BlockSpec(memory_space=pltpu.VMEM)] * n_in,
        out_specs=jax.tree.map(lambda _: pl.BlockSpec(memory_space=pltpu.VMEM), out_shape),
        scratch_shapes=scratch,
        compiler_params=pltpu.CompilerParams(vmem_limit_bytes=32 * 1024 * 1024),
    )


def body(child_inv, child_panel, child_rhs, anc_tiles, root_inv, root_rhs):
    inv, panel, rhs, anc = child_inv[0], child_panel[0], child_rhs[0], anc_tiles[0]
    y, core = lax.axis_index("y"), lax.axis_index("core")
    leaf, zlo = lax.axis_index("leaf"), lax.axis_index("zlo")
    rows = root_rhs.shape[0]
    half = rhs.shape[1] // CORE
    width = half // ZLO
    few = width // LEAF

    def source(to_leaf, to_zlo, j):
        return (to_zlo % LEAF) * ZLO + 2 * to_leaf + (j if to_zlo < LEAF else 1 - j)

    root_own = [
        lax.ppermute(
            root_inv,
            ("leaf", "zlo"),
            [(source(t, s, j), t * ZLO + s) for t in range(LEAF) for s in range(ZLO)],
        )
        for j in range(2)
    ]
    n = inv.shape[0]
    packed = jnp.concatenate([inv[:, i:i + n] for i in range(0, inv.shape[1], n)] + [panel], axis=0)
    packed = lax.all_gather(packed, ("core", "zlo"), axis=0, tiled=False)

    part = dot(rhs, inv, ((0,), (1,))).astype(BF).reshape(CORE, half, n)
    chunk = lax.dynamic_slice_in_dim(
        root_rhs.reshape(rows, CORE, ZLO, width), zlo, 1, axis=2
    )[:, :, 0]
    chunk = jnp.transpose(chunk, (1, 2, 0)).reshape(CORE, width * rows // n, n)
    names = jnp.zeros((16, n), BF).at[:, :2].set(anc.astype(BF)[None])
    local_part = jnp.concatenate([panel, names], axis=0)
    local_part = jnp.broadcast_to(local_part[None], (CORE,) + local_part.shape)
    first = exchange(jnp.concatenate([part, chunk, local_part], axis=1), "core")
    at = [half, half + chunk.shape[1], half + chunk.shape[1] + panel.shape[0]]
    forward = total(share(total(first[:, :at[0]]).astype(BF), "y", Y)).astype(BF)
    side = first[:, at[0]:at[1]].reshape(CORE, width, rows)
    side_own = jnp.where(core == 0, side[0], side[1])
    side_oth = jnp.where(core == 0, side[1], side[0])
    panel_y = first[:, at[1]:at[2]].reshape(-1, n)
    anc_y = first[:, at[2], :2].reshape(-1)

    update = dot(forward, panel_y, ((1,), (1,))).astype(BF)
    span = update.shape[1]
    both = jnp.concatenate([update, forward], axis=1).reshape(ZLO, width, -1)
    both = exchange(both, "zlo")
    forward_all = jnp.transpose(both[:, :, span:], (1, 0, 2)).reshape(width, -1)
    update = total(both[:, :, :span]).astype(BF)
    update = total(share(update, "zhi", ZHI)).astype(BF)
    root_own, update = lax.optimization_barrier((root_own, update))
    root_own = jnp.concatenate(root_own, axis=0)
    root_oth = lax.ppermute(root_own, "core", [(0, 1), (1, 0)])
    names = jnp.zeros((16, span), BF).at[:, :4].set(anc_y[None])
    update = share(jnp.concatenate([update, names], axis=0), "leaf", LEAF)
    slots = update[:, width, :4].reshape(-1).astype(jnp.int32)
    slots = lax.rem(slots - y * 16 + core * 8, 16)

    root_part = call(
        place_kernel,
        jax.ShapeDtypeStruct((width, root_own.shape[0]), BF),
        [pltpu.VMEM((width, 2 * rows), F32)],
        5,
    )(slots, update, side_own, side_oth, root_own, root_oth)
    sol = call(
        spread_kernel,
        jax.ShapeDtypeStruct((LEAF, 2 * width, span), BF),
        [pltpu.VMEM((width, 2 * rows), F32)],
        3,
    )(slots, share(root_part, "y", Y), root_own, root_oth)
    sol = total(exchange(sol, "leaf")).astype(BF)
    picked, root = sol[:width], sol[width:]
    packed, picked = lax.optimization_barrier((packed, picked))
    inv_all = packed[:, :inv.size // n].reshape(CORE, ZLO, -1, n, n)
    inv_all = jnp.transpose(inv_all, (0, 1, 3, 2, 4)).reshape(CORE, ZLO * n, inv.shape[1])
    panel_all = packed[:, inv.size // n:].reshape(CORE, ZLO, -1, n)
    panel_all = jnp.transpose(panel_all, (1, 0, 2, 3)).reshape(ZLO, -1, n)
    picked = total(share(picked, "zhi", ZHI)).astype(BF)

    correction = jnp.concatenate(
        [dot(picked, panel_all[z], ((1,), (0,))) for z in range(ZLO)], axis=1
    ).astype(BF)
    correction = total(share(correction, "y", Y)).astype(BF)
    residue = (forward_all.astype(F32) - correction.astype(F32)).astype(BF)
    child = jnp.stack([dot(inv_all[c], residue, ((0,), (1,))) for c in range(CORE)]).astype(BF)

    cols = ZHI * ZLO
    child = jnp.transpose(child.reshape(CORE, cols, -1, width), (1, 0, 2, 3)).reshape(cols, -1)
    n_child = child.shape[1]
    root = jnp.transpose(root.reshape(CORE, 2, few, span), (0, 2, 1, 3)).reshape(CORE, few, rows)
    root = jnp.stack([jnp.where(core == 0, root[0], root[1]), jnp.where(core == 0, root[1], root[0])])
    root = jnp.transpose(root.reshape(CORE, few, cols, -1), (2, 0, 1, 3)).reshape(cols, -1)
    out = exchange(jnp.concatenate([child, root], axis=1).reshape(cols, -1, TILE), Z)
    out = total(out.reshape(ZHI, ZLO, -1)).astype(BF)
    child = jnp.transpose(out[:, :n_child].reshape(ZLO, CORE, -1), (1, 0, 2)).reshape(CORE, -1)
    root = jnp.transpose(out[:, n_child:].reshape(ZLO, CORE, -1), (1, 0, 2)).reshape(CORE, -1)
    n_child = child.shape[1]
    out = jnp.concatenate([child, root], axis=1)
    out = jnp.broadcast_to(out[None], (LEAF,) + out.shape).reshape(LEAF * CORE, -1, TILE)
    out = exchange(out, ("leaf", "core")).reshape(LEAF, CORE, -1)
    child = lax.dynamic_index_in_dim(out, leaf, 0, keepdims=False)[:, :n_child]
    child = jnp.transpose(child.reshape(CORE * ZLO, -1, width), (1, 0, 2)).reshape(-1, CORE * half)
    root = out[:, :, n_child:].reshape(LEAF, CORE, ZLO, few, -1)
    root = jnp.transpose(root, (4, 1, 2, 0, 3)).reshape(-1, CORE * half)
    return child[None], root


def solution(mesh):
    split = Mesh(
        mesh.devices.reshape(LEAF, Y, CORE, ZHI, ZLO), ("leaf", "y", "core", "zhi", "zlo")
    )
    row, col = ("y", "core"), ("zhi", "zlo")
    in_specs = (
        P("leaf", col, row),
        P("leaf", row, col),
        P("leaf", row, None),
        P("leaf", row),
        P(col, row),
        P(row, None),
    )
    out_specs = (P("leaf", row + col, None), P(row + col, None))
    return jax.shard_map(body, mesh=split, in_specs=in_specs, out_specs=out_specs, check_vma=False)
```

```python
import jax
import jax.numpy as jnp
from jax import lax
from jax.experimental import pallas as pl
from jax.experimental.pallas import tpu as pltpu
from jax.sharding import Mesh, PartitionSpec as P

BF = jnp.bfloat16
F32 = jnp.float32
TILE = 128
LEAF, Y, CORE, ZHI, ZLO = 4, 4, 2, 4, 8
Z = ("zhi", "zlo")


def exchange(x, axis):
    return lax.all_to_all(x, axis, 0, 0, tiled=True)


def share(x, axis, n):
    return exchange(jnp.broadcast_to(x[None], (n,) + x.shape), axis)


def total(parts):
    return jnp.sum(parts.astype(F32), axis=0)


def dot(a, b, contract):
    return lax.dot_general(a, b, (contract, ((), ())), preferred_element_type=F32)


def place_kernel(slot_ref, upd_ref, rhs_own, rhs_oth, root_own, root_oth, out_ref, side_ref):
    half = rhs_own.shape[1]
    side_ref[:, :half] = rhs_own[...].astype(F32)
    side_ref[:, half:] = rhs_oth[...].astype(F32)
    width = side_ref.shape[0]
    for k in range(LEAF):
        for u in range(4):
            at = pl.ds(pl.multiple_of(slot_ref[k * 4 + u] * TILE, TILE), TILE)
            side_ref[:, at] = side_ref[:, at] - upd_ref[k, :width, u * TILE:(u + 1) * TILE].astype(F32)
    out = dot(side_ref[:, :half].astype(BF), root_own[...], ((1,), (1,)))
    out = out + dot(side_ref[:, half:].astype(BF), root_oth[...], ((1,), (1,)))
    out_ref[...] = out.astype(BF)


def spread_kernel(slot_ref, parts_ref, root_own, root_oth, out_ref, sol_ref):
    half = root_own.shape[1]
    forward = parts_ref[0].astype(F32)
    for k in range(1, Y):
        forward = forward + parts_ref[k].astype(F32)
    forward = forward.astype(BF)
    sol_ref[:, :half] = dot(forward, root_own[...], ((1,), (0,)))
    sol_ref[:, half:] = dot(forward, root_oth[...], ((1,), (0,)))
    width, span = forward.shape[0], 4 * TILE
    few = width // LEAF
    for k in range(LEAF):
        for u in range(4):
            at = pl.ds(pl.multiple_of(slot_ref[k * 4 + u] * TILE, TILE), TILE)
            out_ref[k, :width, u * TILE:(u + 1) * TILE] = sol_ref[:, at].astype(BF)
        mine = sol_ref[k * few:(k + 1) * few, :]
        mine = jnp.concatenate([mine[:, j * span:(j + 1) * span] for j in range(4)], axis=0)
        out_ref[k, width:, :] = mine.astype(BF)


def call(kernel, out_shape, scratch, n_in):
    return pl.pallas_call(
        kernel,
        out_shape=out_shape,
        in_specs=[pl.BlockSpec(memory_space=pltpu.SMEM)]
        + [pl.BlockSpec(memory_space=pltpu.VMEM)] * n_in,
        out_specs=jax.tree.map(lambda _: pl.BlockSpec(memory_space=pltpu.VMEM), out_shape),
        scratch_shapes=scratch,
        compiler_params=pltpu.CompilerParams(vmem_limit_bytes=32 * 1024 * 1024),
    )


def body(child_inv, child_panel, child_rhs, anc_tiles, root_inv, root_rhs):
    inv, panel, rhs, anc = child_inv[0], child_panel[0], child_rhs[0], anc_tiles[0]
    y, core = lax.axis_index("y"), lax.axis_index("core")
    leaf, zlo = lax.axis_index("leaf"), lax.axis_index("zlo")
    rows = root_rhs.shape[0]
    other = [(0, 1), (1, 0)]
    half = rhs.shape[1] // CORE
    width = half // ZLO
    few = width // LEAF

    n = inv.shape[0]
    part_rows = root_inv.shape[0] // LEAF
    quarter = lax.dynamic_slice_in_dim(root_inv, leaf * part_rows, part_rows, axis=0)
    fold = rows // n
    packed = jnp.concatenate(
        [
            quarter,
            jnp.concatenate([inv[:n // 2], inv[n // 2:]], axis=1),
            jnp.concatenate(jnp.split(panel, fold, axis=0), axis=1),
        ],
        axis=0,
    )
    packed = lax.all_gather(packed, "zlo", axis=0, tiled=False)

    part = dot(rhs, inv, ((0,), (1,))).astype(BF).reshape(CORE, half, n)
    chunk = lax.dynamic_slice_in_dim(
        root_rhs.reshape(rows, CORE, ZLO, width), zlo, 1, axis=2
    )[:, :, 0]
    chunk = jnp.transpose(chunk, (1, 2, 0)).reshape(CORE, width * rows // n, n)
    names = jnp.zeros((16, n), BF).at[:, :2].set(anc.astype(BF)[None])
    local_part = jnp.concatenate([panel, names], axis=0)
    local_part = jnp.broadcast_to(local_part[None], (CORE,) + local_part.shape)
    first = exchange(jnp.concatenate([part, chunk, local_part], axis=1), "core")
    at = [half, half + chunk.shape[1], half + chunk.shape[1] + panel.shape[0]]
    forward = total(share(total(first[:, :at[0]]).astype(BF), "y", Y)).astype(BF)
    side = first[:, at[0]:at[1]].reshape(CORE, width, rows)
    side_own = jnp.where(core == 0, side[0], side[1])
    side_oth = jnp.where(core == 0, side[1], side[0])
    panel_y = first[:, at[1]:at[2]].reshape(-1, n)
    anc_y = first[:, at[2], :2].reshape(-1)

    update = dot(forward, panel_y, ((1,), (1,))).astype(BF)
    span = update.shape[1]
    both = jnp.concatenate([update, forward], axis=1).reshape(ZLO, width, -1)
    both = exchange(both, "zlo")
    forward_all = jnp.transpose(both[:, :, span:], (1, 0, 2)).reshape(width, -1)
    update = total(both[:, :, :span]).astype(BF)
    update = total(share(update, "zhi", ZHI)).astype(BF)
    packed, update = lax.optimization_barrier((packed, update))
    root_own = packed[:, :part_rows].reshape(-1, rows)
    root_oth = lax.ppermute(root_own, "core", other)
    names = jnp.zeros((16, span), BF).at[:, :4].set(anc_y[None])
    update = share(jnp.concatenate([update, names], axis=0), "leaf", LEAF)
    slots = update[:, width, :4].reshape(-1).astype(jnp.int32)
    slots = lax.rem(slots - y * 16 + core * 8, 16)

    root_part = call(
        place_kernel,
        jax.ShapeDtypeStruct((width, root_own.shape[0]), BF),
        [pltpu.VMEM((width, 2 * rows), F32)],
        5,
    )(slots, update, side_own, side_oth, root_own, root_oth)
    pairs = slots.reshape(LEAF, CORE, 2)
    pairs = jnp.where(core == 0, pairs, pairs[:, ::-1]).reshape(-1)
    sol = call(
        spread_kernel,
        jax.ShapeDtypeStruct((LEAF, 2 * width, span), BF),
        [pltpu.VMEM((width, 2 * rows), F32)],
        3,
    )(pairs, share(root_part, "y", Y), root_own, root_oth)
    sol = total(exchange(sol, "leaf")).astype(BF)
    picked, root = sol[:width], sol[width:]
    mine = packed[:, part_rows:]
    packed = (mine, lax.ppermute(mine, "core", other))

    def unpack(x):
        x_inv = jnp.concatenate([x[:, :n // 2, :rows // 2], x[:, :n // 2, rows // 2:]], axis=1)
        x_panel = jnp.transpose(x[:, n // 2:].reshape(ZLO, -1, fold, n), (0, 2, 1, 3))
        return x_inv.reshape(ZLO * n, -1), x_panel.reshape(ZLO, -1, n)

    (inv_own, panel_own), (inv_oth, panel_oth) = unpack(packed[0]), unpack(packed[1])
    inv_own, panel_own, inv_oth, panel_oth, picked = lax.optimization_barrier(
        (inv_own, panel_own, inv_oth, panel_oth, picked)
    )
    picked = total(share(picked, "zhi", ZHI)).astype(BF)

    first, second = picked[:, :span // 2], picked[:, span // 2:]
    correction = jnp.concatenate(
        [
            dot(first, panel_own[z], ((1,), (0,))) + dot(second, panel_oth[z], ((1,), (0,)))
            for z in range(ZLO)
        ],
        axis=1,
    ).astype(BF)
    correction = total(share(correction, "y", Y)).astype(BF)
    residue = (forward_all.astype(F32) - correction.astype(F32)).astype(BF)
    child = [dot(m, residue, ((0,), (1,))).astype(BF) for m in (inv_own, inv_oth)]
    child = jnp.stack(
        [jnp.where(core == 0, child[0], child[1]), jnp.where(core == 0, child[1], child[0])]
    )

    cols = ZHI * ZLO
    child = jnp.transpose(child.reshape(CORE, cols, -1, width), (1, 0, 2, 3)).reshape(cols, -1)
    n_child = child.shape[1]
    root = jnp.transpose(root.reshape(CORE, 2, few, span), (0, 2, 1, 3)).reshape(CORE, few, rows)
    root = jnp.stack([jnp.where(core == 0, root[0], root[1]), jnp.where(core == 0, root[1], root[0])])
    root = jnp.transpose(root.reshape(CORE, few, cols, -1), (2, 0, 1, 3)).reshape(cols, -1)
    out = exchange(jnp.concatenate([child, root], axis=1).reshape(cols, -1, TILE), Z)
    out = total(out.reshape(ZHI, ZLO, -1)).astype(BF)
    child = jnp.transpose(out[:, :n_child].reshape(ZLO, CORE, -1), (1, 0, 2)).reshape(CORE, -1)
    root = jnp.transpose(out[:, n_child:].reshape(ZLO, CORE, -1), (1, 0, 2)).reshape(CORE, -1)
    n_child = child.shape[1]
    out = jnp.concatenate([child, root], axis=1)
    out = jnp.broadcast_to(out[None], (LEAF,) + out.shape).reshape(LEAF * CORE, -1, TILE)
    out = exchange(out, ("leaf", "core")).reshape(LEAF, CORE, -1)
    child = lax.dynamic_index_in_dim(out, leaf, 0, keepdims=False)[:, :n_child]
    child = jnp.transpose(child.reshape(CORE * ZLO, -1, width), (1, 0, 2)).reshape(-1, CORE * half)
    root = out[:, :, n_child:].reshape(LEAF, CORE, ZLO, few, -1)
    root = jnp.transpose(root, (4, 1, 2, 0, 3)).reshape(-1, CORE * half)
    return child[None], root


def solution(mesh):
    split = Mesh(
        mesh.devices.reshape(LEAF, Y, CORE, ZHI, ZLO), ("leaf", "y", "core", "zhi", "zlo")
    )
    row, col = ("y", "core"), ("zhi", "zlo")
    in_specs = (
        P("leaf", col, row),
        P("leaf", row, col),
        P("leaf", row, None),
        P("leaf", row),
        P(col, row),
        P(row, None),
    )
    out_specs = (P("leaf", row + col, None), P(row + col, None))
    return jax.shard_map(body, mesh=split, in_specs=in_specs, out_specs=out_specs, check_vma=False)
```

```python
import jax
import jax.numpy as jnp
from jax import lax
from jax.experimental import pallas as pl
from jax.experimental.pallas import tpu as pltpu
from jax.sharding import Mesh, PartitionSpec as P

BF = jnp.bfloat16
F32 = jnp.float32
TILE = 128
LEAF, Y, CORE, ZHI, ZLO = 4, 4, 2, 4, 8
Z = ("zhi", "zlo")


def exchange(x, axis):
    return lax.all_to_all(x, axis, 0, 0, tiled=True)


def share(x, axis, n):
    return exchange(jnp.broadcast_to(x[None], (n,) + x.shape), axis)


def total(parts):
    return jnp.sum(parts.astype(F32), axis=0)


def dot(a, b, contract):
    return lax.dot_general(a, b, (contract, ((), ())), preferred_element_type=F32)


def place_kernel(slot_ref, upd_ref, rhs_own, rhs_oth, root_own, root_oth, out_ref, side_ref):
    half = rhs_own.shape[1]
    side_ref[:, :half] = rhs_own[...].astype(F32)
    side_ref[:, half:] = rhs_oth[...].astype(F32)
    width = side_ref.shape[0]
    for k in range(LEAF):
        for u in range(4):
            at = pl.ds(pl.multiple_of(slot_ref[k * 4 + u] * TILE, TILE), TILE)
            side_ref[:, at] = side_ref[:, at] - upd_ref[k, :width, u * TILE:(u + 1) * TILE].astype(F32)
    out = dot(side_ref[:, :half].astype(BF), root_own[...], ((1,), (1,)))
    out = out + dot(side_ref[:, half:].astype(BF), root_oth[...], ((1,), (1,)))
    for k in range(Y):
        out_ref[k] = out.astype(BF)


def spread_kernel(slot_ref, parts_ref, root_own, root_oth, out_ref, sol_ref):
    half = root_own.shape[1]
    forward = parts_ref[0].astype(F32)
    for k in range(1, Y):
        forward = forward + parts_ref[k].astype(F32)
    forward = forward.astype(BF)
    sol_ref[:, :half] = dot(forward, root_own[...], ((1,), (0,)))
    sol_ref[:, half:] = dot(forward, root_oth[...], ((1,), (0,)))
    width, span = forward.shape[0], 4 * TILE
    few = width // LEAF
    for k in range(LEAF):
        for u in range(4):
            at = pl.ds(pl.multiple_of(slot_ref[k * 4 + u] * TILE, TILE), TILE)
            out_ref[k, :width, u * TILE:(u + 1) * TILE] = sol_ref[:, at].astype(BF)
        mine = sol_ref[k * few:(k + 1) * few, :]
        mine = jnp.concatenate([mine[:, j * span:(j + 1) * span] for j in range(4)], axis=0)
        out_ref[k, width:, :] = mine.astype(BF)


def pack_kernel(inv_ref, panel_ref, out_ref):
    n, lanes = inv_ref.shape
    out_ref[:n] = inv_ref[...]
    fold = lanes // TILE
    few = panel_ref.shape[0] // fold
    for f in range(fold):
        out_ref[n:, f * TILE:(f + 1) * TILE] = panel_ref[f * few:(f + 1) * few]


def correct_kernel(parts_ref, own_ref, oth_ref, out_ref):
    picked = parts_ref[0].astype(F32)
    for k in range(1, ZHI):
        picked = picked + parts_ref[k].astype(F32)
    picked = picked.astype(BF)
    half = picked.shape[1] // 2
    n, lanes = TILE, own_ref.shape[2]
    for z in range(ZLO):
        out = 0.0
        for i, ref in enumerate((own_ref, oth_ref)):
            panel = jnp.concatenate([ref[z, n:, f:f + TILE] for f in range(0, lanes, TILE)], axis=0)
            out = out + dot(picked[:, i * half:(i + 1) * half], panel, ((1,), (0,)))
        for k in range(Y):
            out_ref[k, :, z * n:(z + 1) * n] = out.astype(BF)


def solve_kernel(core_ref, forward_ref, parts_ref, own_ref, oth_ref, out_ref):
    correction = parts_ref[0].astype(F32)
    for k in range(1, Y):
        correction = correction + parts_ref[k].astype(F32)
    residue = forward_ref[...].astype(F32) - correction.astype(BF).astype(F32)
    residue = residue.astype(BF)
    n = TILE
    core = core_ref[0]
    for i, ref in enumerate((own_ref, oth_ref)):
        inv = ref[:, :n, :].reshape(ZLO * n, ref.shape[2])
        out_ref[(core + i) % CORE] = dot(inv, residue, ((0,), (1,))).astype(BF)


def call(kernel, out_shape, scratch, n_in, n_scalar=1):
    return pl.pallas_call(
        kernel,
        out_shape=out_shape,
        in_specs=[pl.BlockSpec(memory_space=pltpu.SMEM)] * n_scalar
        + [pl.BlockSpec(memory_space=pltpu.VMEM)] * n_in,
        out_specs=jax.tree.map(lambda _: pl.BlockSpec(memory_space=pltpu.VMEM), out_shape),
        scratch_shapes=scratch,
        compiler_params=pltpu.CompilerParams(vmem_limit_bytes=32 * 1024 * 1024),
    )


def body(child_inv, child_panel, child_rhs, anc_tiles, root_inv, root_rhs):
    inv, panel, rhs, anc = child_inv[0], child_panel[0], child_rhs[0], anc_tiles[0]
    y, core = lax.axis_index("y"), lax.axis_index("core")
    leaf, zlo = lax.axis_index("leaf"), lax.axis_index("zlo")
    rows = root_rhs.shape[0]
    other = [(0, 1), (1, 0)]
    half = rhs.shape[1] // CORE
    width = half // ZLO
    few = width // LEAF

    n = inv.shape[0]
    part_rows = root_inv.shape[0] // LEAF
    quarter = lax.dynamic_slice_in_dim(root_inv, leaf * part_rows, part_rows, axis=0)
    root_own = lax.all_gather(quarter, "zlo", axis=0, tiled=True)
    packed = call(
        pack_kernel, jax.ShapeDtypeStruct((n + panel.size // inv.shape[1], inv.shape[1]), BF), [], 2, 0
    )(inv, panel)
    packed = lax.all_gather(packed, "zlo", axis=0, tiled=False)

    part = dot(rhs, inv, ((0,), (1,))).astype(BF).reshape(CORE, half, n)
    chunk = lax.dynamic_slice_in_dim(
        root_rhs.reshape(rows, CORE, ZLO, width), zlo, 1, axis=2
    )[:, :, 0]
    chunk = jnp.transpose(chunk, (1, 2, 0)).reshape(CORE, width * rows // n, n)
    names = jnp.zeros((16, n), BF).at[:, :2].set(anc.astype(BF)[None])
    local_part = jnp.concatenate([panel, names], axis=0)
    local_part = jnp.broadcast_to(local_part[None], (CORE,) + local_part.shape)
    first = exchange(jnp.concatenate([part, chunk, local_part], axis=1), "core")
    at = [half, half + chunk.shape[1], half + chunk.shape[1] + panel.shape[0]]
    forward = total(share(total(first[:, :at[0]]).astype(BF), "y", Y)).astype(BF)
    side = first[:, at[0]:at[1]].reshape(CORE, width, rows)
    side_own = jnp.where(core == 0, side[0], side[1])
    side_oth = jnp.where(core == 0, side[1], side[0])
    panel_y = first[:, at[1]:at[2]].reshape(-1, n)
    anc_y = first[:, at[2], :2].reshape(-1)

    update = dot(forward, panel_y, ((1,), (1,))).astype(BF)
    span = update.shape[1]
    both = jnp.concatenate([update, forward], axis=1).reshape(ZLO, width, -1)
    both = exchange(both, "zlo")
    forward_all = jnp.transpose(both[:, :, span:], (1, 0, 2)).reshape(width, -1)
    update = total(both[:, :, :span]).astype(BF)
    update = total(share(update, "zhi", ZHI)).astype(BF)
    root_own, update = lax.optimization_barrier((root_own, update))
    root_oth = lax.ppermute(root_own, "core", other)
    names = jnp.zeros((16, span), BF).at[:, :4].set(anc_y[None])
    update = share(jnp.concatenate([update, names], axis=0), "leaf", LEAF)
    slots = update[:, width, :4].reshape(-1).astype(jnp.int32)
    slots = lax.rem(slots - y * 16 + core * 8, 16)

    root_part = call(
        place_kernel,
        jax.ShapeDtypeStruct((Y, width, root_own.shape[0]), BF),
        [pltpu.VMEM((width, 2 * rows), F32)],
        5,
    )(slots, update, side_own, side_oth, root_own, root_oth)
    packed, root_part = lax.optimization_barrier((packed, root_part))
    packed_oth = lax.ppermute(packed, "core", other)
    pairs = slots.reshape(LEAF, CORE, 2)
    pairs = jnp.where(core == 0, pairs, pairs[:, ::-1]).reshape(-1)
    sol = call(
        spread_kernel,
        jax.ShapeDtypeStruct((LEAF, 2 * width, span), BF),
        [pltpu.VMEM((width, 2 * rows), F32)],
        3,
    )(pairs, exchange(root_part, "y"), root_own, root_oth)
    sol = total(exchange(sol, "leaf")).astype(BF)
    picked, root = sol[:width], sol[width:]
    correction = call(
        correct_kernel, jax.ShapeDtypeStruct((Y, width, ZLO * n), BF), [], 3, 0
    )(share(picked, "zhi", ZHI), packed, packed_oth)
    child = call(
        solve_kernel, jax.ShapeDtypeStruct((CORE, inv.shape[1], width), BF), [], 4
    )(jnp.array([core], jnp.int32), forward_all, exchange(correction, "y"), packed, packed_oth)

    cols = ZHI * ZLO
    child = jnp.transpose(child.reshape(CORE, cols, -1, width), (1, 0, 2, 3)).reshape(cols, -1)
    n_child = child.shape[1]
    root = jnp.transpose(root.reshape(CORE, 2, few, span), (0, 2, 1, 3)).reshape(CORE, few, rows)
    root = jnp.stack([jnp.where(core == 0, root[0], root[1]), jnp.where(core == 0, root[1], root[0])])
    root = jnp.transpose(root.reshape(CORE, few, cols, -1), (2, 0, 1, 3)).reshape(cols, -1)
    out = exchange(jnp.concatenate([child, root], axis=1).reshape(cols, -1, TILE), Z)
    out = total(out.reshape(ZHI, ZLO, -1)).astype(BF)
    child = jnp.transpose(out[:, :n_child].reshape(ZLO, CORE, -1), (1, 0, 2)).reshape(CORE, -1)
    root = jnp.transpose(out[:, n_child:].reshape(ZLO, CORE, -1), (1, 0, 2)).reshape(CORE, -1)
    n_child = child.shape[1]
    out = jnp.concatenate([child, root], axis=1)
    out = jnp.broadcast_to(out[None], (LEAF,) + out.shape).reshape(LEAF * CORE, -1, TILE)
    out = exchange(out, ("leaf", "core")).reshape(LEAF, CORE, -1)
    child = lax.dynamic_index_in_dim(out, leaf, 0, keepdims=False)[:, :n_child]
    child = jnp.transpose(child.reshape(CORE * ZLO, -1, width), (1, 0, 2)).reshape(-1, CORE * half)
    root = out[:, :, n_child:].reshape(LEAF, CORE, ZLO, few, -1)
    root = jnp.transpose(root, (4, 1, 2, 0, 3)).reshape(-1, CORE * half)
    return child[None], root


def solution(mesh):
    split = Mesh(
        mesh.devices.reshape(LEAF, Y, CORE, ZHI, ZLO), ("leaf", "y", "core", "zhi", "zlo")
    )
    row, col = ("y", "core"), ("zhi", "zlo")
    in_specs = (
        P("leaf", col, row),
        P("leaf", row, col),
        P("leaf", row, None),
        P("leaf", row),
        P(col, row),
        P(row, None),
    )
    out_specs = (P("leaf", row + col, None), P(row + col, None))
    return jax.shard_map(body, mesh=split, in_specs=in_specs, out_specs=out_specs, check_vma=False)
```

```python
import jax
import jax.numpy as jnp
from jax import lax
from jax.experimental import pallas as pl
from jax.experimental.pallas import tpu as pltpu
from jax.sharding import Mesh, PartitionSpec as P

BF = jnp.bfloat16
F32 = jnp.float32
TILE = 128
LEAF, Y, CORE, ZHI, ZLO = 4, 4, 2, 4, 8
Z = ("zhi", "zlo")


def exchange(x, axis):
    return lax.all_to_all(x, axis, 0, 0, tiled=True)


def share(x, axis, n):
    return exchange(jnp.broadcast_to(x[None], (n,) + x.shape), axis)


def total(parts):
    return jnp.sum(parts.astype(F32), axis=0)


def dot(a, b, contract):
    return lax.dot_general(a, b, (contract, ((), ())), preferred_element_type=F32)


QUARTER, INV = 64, 128


def pack_kernel(leaf_ref, root_ref, inv_ref, panel_ref, out_ref):
    lanes = inv_ref.shape[1]
    at = pl.ds(pl.multiple_of(leaf_ref[0] * QUARTER, QUARTER), QUARTER)
    out_ref[:QUARTER] = root_ref[at, :lanes]
    out_ref[QUARTER:2 * QUARTER] = root_ref[at, lanes:]
    start = 2 * QUARTER
    out_ref[start:start + INV] = inv_ref[...]
    fold = lanes // TILE
    few = panel_ref.shape[0] // fold
    for f in range(fold):
        out_ref[start + INV:, f * TILE:(f + 1) * TILE] = panel_ref[f * few:(f + 1) * few]


def root_half(ref, j):
    return ref[:, j * QUARTER:(j + 1) * QUARTER, :].reshape(ZLO * QUARTER, ref.shape[2])


def place_kernel(slot_ref, upd_ref, rhs_own, rhs_oth, own_ref, oth_ref, out_ref, side_ref):
    half = rhs_own.shape[1]
    lanes = own_ref.shape[2]
    side_ref[:, :half] = rhs_own[...].astype(F32)
    side_ref[:, half:] = rhs_oth[...].astype(F32)
    width = side_ref.shape[0]
    for k in range(LEAF):
        for u in range(4):
            at = pl.ds(pl.multiple_of(slot_ref[k * 4 + u] * TILE, TILE), TILE)
            side_ref[:, at] = side_ref[:, at] - upd_ref[k, :width, u * TILE:(u + 1) * TILE].astype(F32)
    out = 0.0
    for i in range(4):
        side = side_ref[:, i * lanes:(i + 1) * lanes].astype(BF)
        out = out + dot(side, root_half((own_ref, oth_ref)[i // 2], i % 2), ((1,), (1,)))
    for k in range(Y):
        out_ref[k] = out.astype(BF)


def spread_kernel(slot_ref, parts_ref, own_ref, oth_ref, out_ref, sol_ref):
    lanes = own_ref.shape[2]
    forward = parts_ref[0].astype(F32)
    for k in range(1, Y):
        forward = forward + parts_ref[k].astype(F32)
    forward = forward.astype(BF)
    for i in range(4):
        root = root_half((own_ref, oth_ref)[i // 2], i % 2)
        sol_ref[:, i * lanes:(i + 1) * lanes] = dot(forward, root, ((1,), (0,)))
    width, span = forward.shape[0], 4 * TILE
    few = width // LEAF
    for k in range(LEAF):
        for u in range(4):
            at = pl.ds(pl.multiple_of(slot_ref[k * 4 + u] * TILE, TILE), TILE)
            out_ref[k, :width, u * TILE:(u + 1) * TILE] = sol_ref[:, at].astype(BF)
        mine = sol_ref[k * few:(k + 1) * few, :]
        mine = jnp.concatenate([mine[:, j * span:(j + 1) * span] for j in range(4)], axis=0)
        out_ref[k, width:, :] = mine.astype(BF)


def correct_kernel(parts_ref, own_ref, oth_ref, out_ref):
    picked = parts_ref[0].astype(F32)
    for k in range(1, ZHI):
        picked = picked + parts_ref[k].astype(F32)
    picked = picked.astype(BF)
    half = picked.shape[1] // 2
    n, lanes = TILE, own_ref.shape[2]
    start = 2 * QUARTER + INV
    for z in range(ZLO):
        out = 0.0
        for i, ref in enumerate((own_ref, oth_ref)):
            panel = jnp.concatenate([ref[z, start:, f:f + TILE] for f in range(0, lanes, TILE)], axis=0)
            out = out + dot(picked[:, i * half:(i + 1) * half], panel, ((1,), (0,)))
        for k in range(Y):
            out_ref[k, :, z * n:(z + 1) * n] = out.astype(BF)


def solve_kernel(core_ref, forward_ref, parts_ref, own_ref, oth_ref, out_ref):
    correction = parts_ref[0].astype(F32)
    for k in range(1, Y):
        correction = correction + parts_ref[k].astype(F32)
    residue = forward_ref[...].astype(F32) - correction.astype(BF).astype(F32)
    residue = residue.astype(BF)
    n = TILE
    core = core_ref[0]
    for i, ref in enumerate((own_ref, oth_ref)):
        inv = ref[:, 2 * QUARTER:2 * QUARTER + n, :].reshape(ZLO * n, ref.shape[2])
        out_ref[(core + i) % CORE] = dot(inv, residue, ((0,), (1,))).astype(BF)


def call(kernel, out_shape, scratch, n_in, n_scalar=1):
    return pl.pallas_call(
        kernel,
        out_shape=out_shape,
        in_specs=[pl.BlockSpec(memory_space=pltpu.SMEM)] * n_scalar
        + [pl.BlockSpec(memory_space=pltpu.VMEM)] * n_in,
        out_specs=jax.tree.map(lambda _: pl.BlockSpec(memory_space=pltpu.VMEM), out_shape),
        scratch_shapes=scratch,
        compiler_params=pltpu.CompilerParams(vmem_limit_bytes=32 * 1024 * 1024),
    )


def body(child_inv, child_panel, child_rhs, anc_tiles, root_inv, root_rhs):
    inv, panel, rhs, anc = child_inv[0], child_panel[0], child_rhs[0], anc_tiles[0]
    y, core = lax.axis_index("y"), lax.axis_index("core")
    leaf, zlo = lax.axis_index("leaf"), lax.axis_index("zlo")
    rows = root_rhs.shape[0]
    other = [(0, 1), (1, 0)]
    half = rhs.shape[1] // CORE
    width = half // ZLO
    few = width // LEAF

    n = inv.shape[0]
    packed_rows = 2 * QUARTER + INV + panel.size // inv.shape[1]
    packed = call(pack_kernel, jax.ShapeDtypeStruct((packed_rows, inv.shape[1]), BF), [], 3)(
        jnp.array([leaf], jnp.int32), root_inv, inv, panel
    )
    packed = lax.all_gather(packed, "zlo", axis=0, tiled=False)

    part = dot(rhs, inv, ((0,), (1,))).astype(BF).reshape(CORE, half, n)
    chunk = lax.dynamic_slice_in_dim(
        root_rhs.reshape(rows, CORE, ZLO, width), zlo, 1, axis=2
    )[:, :, 0]
    chunk = jnp.transpose(chunk, (1, 2, 0)).reshape(CORE, width * rows // n, n)
    names = jnp.zeros((16, n), BF).at[:, :2].set(anc.astype(BF)[None])
    local_part = jnp.concatenate([panel, names], axis=0)
    local_part = jnp.broadcast_to(local_part[None], (CORE,) + local_part.shape)
    first = exchange(jnp.concatenate([part, chunk, local_part], axis=1), "core")
    at = [half, half + chunk.shape[1], half + chunk.shape[1] + panel.shape[0]]
    forward = total(share(total(first[:, :at[0]]).astype(BF), "y", Y)).astype(BF)
    side = first[:, at[0]:at[1]].reshape(CORE, width, rows)
    side_own = jnp.where(core == 0, side[0], side[1])
    side_oth = jnp.where(core == 0, side[1], side[0])
    panel_y = first[:, at[1]:at[2]].reshape(-1, n)
    anc_y = first[:, at[2], :2].reshape(-1)

    update = dot(forward, panel_y, ((1,), (1,))).astype(BF)
    span = update.shape[1]
    both = jnp.concatenate([update, forward], axis=1).reshape(ZLO, width, -1)
    both = exchange(both, "zlo")
    forward_all = jnp.transpose(both[:, :, span:], (1, 0, 2)).reshape(width, -1)
    update = total(both[:, :, :span]).astype(BF)
    update = total(share(update, "zhi", ZHI)).astype(BF)
    packed, update = lax.optimization_barrier((packed, update))
    packed_oth = lax.ppermute(packed, "core", other)
    names = jnp.zeros((16, span), BF).at[:, :4].set(anc_y[None])
    update = share(jnp.concatenate([update, names], axis=0), "leaf", LEAF)
    slots = update[:, width, :4].reshape(-1).astype(jnp.int32)
    slots = lax.rem(slots - y * 16 + core * 8, 16)

    root_part = call(
        place_kernel,
        jax.ShapeDtypeStruct((Y, width, ZLO * QUARTER), BF),
        [pltpu.VMEM((width, 2 * rows), F32)],
        5,
    )(slots, update, side_own, side_oth, packed, packed_oth)
    pairs = slots.reshape(LEAF, CORE, 2)
    pairs = jnp.where(core == 0, pairs, pairs[:, ::-1]).reshape(-1)
    sol = call(
        spread_kernel,
        jax.ShapeDtypeStruct((LEAF, 2 * width, span), BF),
        [pltpu.VMEM((width, 2 * rows), F32)],
        3,
    )(pairs, exchange(root_part, "y"), packed, packed_oth)
    sol = total(exchange(sol, "leaf")).astype(BF)
    picked, root = sol[:width], sol[width:]
    correction = call(
        correct_kernel, jax.ShapeDtypeStruct((Y, width, ZLO * n), BF), [], 3, 0
    )(share(picked, "zhi", ZHI), packed, packed_oth)
    child = call(
        solve_kernel, jax.ShapeDtypeStruct((CORE, inv.shape[1], width), BF), [], 4
    )(jnp.array([core], jnp.int32), forward_all, exchange(correction, "y"), packed, packed_oth)

    cols = ZHI * ZLO
    child = jnp.transpose(child.reshape(CORE, cols, -1, width), (1, 0, 2, 3)).reshape(cols, -1)
    n_child = child.shape[1]
    root = jnp.transpose(root.reshape(CORE, 2, few, span), (0, 2, 1, 3)).reshape(CORE, few, rows)
    root = jnp.stack([jnp.where(core == 0, root[0], root[1]), jnp.where(core == 0, root[1], root[0])])
    root = jnp.transpose(root.reshape(CORE, few, cols, -1), (2, 0, 1, 3)).reshape(cols, -1)
    out = exchange(jnp.concatenate([child, root], axis=1).reshape(cols, -1, TILE), Z)
    out = total(out.reshape(ZHI, ZLO, -1)).astype(BF)
    child = jnp.transpose(out[:, :n_child].reshape(ZLO, CORE, -1), (1, 0, 2)).reshape(CORE, -1)
    root = jnp.transpose(out[:, n_child:].reshape(ZLO, CORE, -1), (1, 0, 2)).reshape(CORE, -1)
    n_child = child.shape[1]
    out = jnp.concatenate([child, root], axis=1)
    out = jnp.broadcast_to(out[None], (LEAF,) + out.shape).reshape(LEAF * CORE, -1, TILE)
    out = exchange(out, ("leaf", "core")).reshape(LEAF, CORE, -1)
    child = lax.dynamic_index_in_dim(out, leaf, 0, keepdims=False)[:, :n_child]
    child = jnp.transpose(child.reshape(CORE * ZLO, -1, width), (1, 0, 2)).reshape(-1, CORE * half)
    root = out[:, :, n_child:].reshape(LEAF, CORE, ZLO, few, -1)
    root = jnp.transpose(root, (4, 1, 2, 0, 3)).reshape(-1, CORE * half)
    return child[None], root


def solution(mesh):
    split = Mesh(
        mesh.devices.reshape(LEAF, Y, CORE, ZHI, ZLO), ("leaf", "y", "core", "zhi", "zlo")
    )
    row, col = ("y", "core"), ("zhi", "zlo")
    in_specs = (
        P("leaf", col, row),
        P("leaf", row, col),
        P("leaf", row, None),
        P("leaf", row),
        P(col, row),
        P(row, None),
    )
    out_specs = (P("leaf", row + col, None), P(row + col, None))
    return jax.shard_map(body, mesh=split, in_specs=in_specs, out_specs=out_specs, check_vma=False)
```

```python
import jax
import jax.numpy as jnp
from jax import lax
from jax.experimental import pallas as pl
from jax.experimental.pallas import tpu as pltpu
from jax.sharding import Mesh, PartitionSpec as P

BF = jnp.bfloat16
F32 = jnp.float32
TILE = 128
LEAF, Y, CORE, ZHI, ZLO = 4, 4, 2, 4, 8
Z = ("zhi", "zlo")


def exchange(x, axis):
    return lax.all_to_all(x, axis, 0, 0, tiled=True)


def share(x, axis, n):
    return exchange(jnp.broadcast_to(x[None], (n,) + x.shape), axis)


def total(parts):
    return jnp.sum(parts.astype(F32), axis=0)


def dot(a, b, contract):
    return lax.dot_general(a, b, (contract, ((), ())), preferred_element_type=F32)


QUARTER = 64


def pack_kernel(leaf_ref, root_ref, panel_ref, out_ref):
    lanes = out_ref.shape[1]
    at = pl.ds(pl.multiple_of(leaf_ref[0] * QUARTER, QUARTER), QUARTER)
    out_ref[:QUARTER] = root_ref[at, :lanes]
    out_ref[QUARTER:2 * QUARTER] = root_ref[at, lanes:]
    start = 2 * QUARTER
    fold = lanes // TILE
    few = panel_ref.shape[0] // fold
    for f in range(fold):
        out_ref[start:, f * TILE:(f + 1) * TILE] = panel_ref[f * few:(f + 1) * few]


def root_half(ref, j):
    return ref[:, j * QUARTER:(j + 1) * QUARTER, :].reshape(ZLO * QUARTER, ref.shape[2])


def place_kernel(slot_ref, upd_ref, rhs_own, rhs_oth, own_ref, oth_ref, out_ref, side_ref):
    half = rhs_own.shape[1]
    lanes = own_ref.shape[2]
    side_ref[:, :half] = rhs_own[...].astype(F32)
    side_ref[:, half:] = rhs_oth[...].astype(F32)
    width = side_ref.shape[0]
    for k in range(LEAF):
        for u in range(4):
            at = pl.ds(pl.multiple_of(slot_ref[k * 4 + u] * TILE, TILE), TILE)
            side_ref[:, at] = side_ref[:, at] - upd_ref[k, :width, u * TILE:(u + 1) * TILE].astype(F32)
    out = 0.0
    for i in range(4):
        side = side_ref[:, i * lanes:(i + 1) * lanes].astype(BF)
        out = out + dot(side, root_half((own_ref, oth_ref)[i // 2], i % 2), ((1,), (1,)))
    for k in range(Y):
        out_ref[k] = out.astype(BF)


def spread_kernel(slot_ref, parts_ref, own_ref, oth_ref, out_ref, sol_ref):
    lanes = own_ref.shape[2]
    forward = parts_ref[0].astype(F32)
    for k in range(1, Y):
        forward = forward + parts_ref[k].astype(F32)
    forward = forward.astype(BF)
    for i in range(4):
        root = root_half((own_ref, oth_ref)[i // 2], i % 2)
        sol_ref[:, i * lanes:(i + 1) * lanes] = dot(forward, root, ((1,), (0,)))
    width, span = forward.shape[0], 4 * TILE
    few = width // LEAF
    for k in range(LEAF):
        for u in range(4):
            at = pl.ds(pl.multiple_of(slot_ref[k * 4 + u] * TILE, TILE), TILE)
            out_ref[k, :width, u * TILE:(u + 1) * TILE] = sol_ref[:, at].astype(BF)
        mine = sol_ref[k * few:(k + 1) * few, :]
        mine = jnp.concatenate([mine[:, j * span:(j + 1) * span] for j in range(4)], axis=0)
        out_ref[k, width:, :] = mine.astype(BF)


def correct_kernel(parts_ref, own_ref, oth_ref, out_ref):
    picked = parts_ref[0].astype(F32)
    for k in range(1, ZHI):
        picked = picked + parts_ref[k].astype(F32)
    picked = picked.astype(BF)
    half = picked.shape[1] // 2
    n, lanes = TILE, own_ref.shape[2]
    for z in range(ZLO):
        out = 0.0
        for i, ref in enumerate((own_ref, oth_ref)):
            panel = jnp.concatenate([ref[z, :, f:f + TILE] for f in range(0, lanes, TILE)], axis=0)
            out = out + dot(picked[:, i * half:(i + 1) * half], panel, ((1,), (0,)))
        for k in range(Y):
            out_ref[k, :, z * n:(z + 1) * n] = out.astype(BF)


def solve_kernel(core_ref, forward_ref, parts_ref, own_ref, oth_ref, out_ref):
    correction = parts_ref[0].astype(F32)
    for k in range(1, Y):
        correction = correction + parts_ref[k].astype(F32)
    residue = forward_ref[...].astype(F32) - correction.astype(BF).astype(F32)
    residue = residue.astype(BF)
    n = TILE
    core = core_ref[0]
    for i, ref in enumerate((own_ref, oth_ref)):
        inv = ref[...].reshape(ZLO * n, ref.shape[2])
        out_ref[(core + i) % CORE] = dot(inv, residue, ((0,), (1,))).astype(BF)


def call(kernel, out_shape, scratch, inputs, scalars=(), blocks=()):
    def whole(x):
        return pl.BlockSpec(x.shape, lambda i: (0,) * len(x.shape))

    return pl.pallas_call(
        kernel,
        grid=(1,),
        out_shape=out_shape,
        in_specs=[pl.BlockSpec(memory_space=pltpu.SMEM)] * len(scalars)
        + [whole(x) for x in inputs[:len(inputs) - len(blocks)]]
        + list(blocks),
        out_specs=whole(out_shape),
        scratch_shapes=scratch,
        compiler_params=pltpu.CompilerParams(vmem_limit_bytes=40 * 1024 * 1024),
    )(*scalars, *inputs)


def body(child_inv, child_panel, child_rhs, anc_tiles, root_inv, root_rhs):
    inv, panel, rhs, anc = child_inv[0], child_panel[0], child_rhs[0], anc_tiles[0]
    y, core = lax.axis_index("y"), lax.axis_index("core")
    leaf, zlo = lax.axis_index("leaf"), lax.axis_index("zlo")
    rows = root_rhs.shape[0]
    other = [(0, 1), (1, 0)]
    half = rhs.shape[1] // CORE
    width = half // ZLO
    few = width // LEAF

    n = inv.shape[0]
    lanes = inv.shape[1]
    packed_rows = 2 * QUARTER + panel.size // lanes
    packed = call(
        pack_kernel,
        jax.ShapeDtypeStruct((packed_rows, lanes), BF),
        [],
        (root_inv, panel),
        (jnp.array([leaf], jnp.int32),),
    )
    packed = lax.all_gather(packed, "zlo", axis=0, tiled=False)
    inv_own = lax.all_gather(inv, "zlo", axis=0, tiled=False)
    root_block = pl.BlockSpec((ZLO, 2 * QUARTER, lanes), lambda i: (0, 0, 0))
    panel_block = pl.BlockSpec((ZLO, QUARTER, lanes), lambda i: (0, 2, 0))

    part = dot(rhs, inv, ((0,), (1,))).astype(BF).reshape(CORE, half, n)
    chunk = lax.dynamic_slice_in_dim(
        root_rhs.reshape(rows, CORE, ZLO, width), zlo, 1, axis=2
    )[:, :, 0]
    chunk = jnp.transpose(chunk, (1, 2, 0)).reshape(CORE, width * rows // n, n)
    names = jnp.zeros((16, n), BF).at[:, :2].set(anc.astype(BF)[None])
    local_part = jnp.concatenate([panel, names], axis=0)
    local_part = jnp.broadcast_to(local_part[None], (CORE,) + local_part.shape)
    first = exchange(jnp.concatenate([part, chunk, local_part], axis=1), "core")
    at = [half, half + chunk.shape[1], half + chunk.shape[1] + panel.shape[0]]
    forward = total(share(total(first[:, :at[0]]).astype(BF), "y", Y)).astype(BF)
    side = first[:, at[0]:at[1]].reshape(CORE, width, rows)
    side_own = jnp.where(core == 0, side[0], side[1])
    side_oth = jnp.where(core == 0, side[1], side[0])
    panel_y = first[:, at[1]:at[2]].reshape(-1, n)
    anc_y = first[:, at[2], :2].reshape(-1)

    update = dot(forward, panel_y, ((1,), (1,))).astype(BF)
    span = update.shape[1]
    both = jnp.concatenate([update, forward], axis=1).reshape(ZLO, width, -1)
    both = exchange(both, "zlo")
    forward_all = jnp.transpose(both[:, :, span:], (1, 0, 2)).reshape(width, -1)
    update = total(both[:, :, :span]).astype(BF)
    update = total(share(update, "zhi", ZHI)).astype(BF)
    packed, update = lax.optimization_barrier((packed, update))
    packed_oth = lax.ppermute(packed, "core", other)
    names = jnp.zeros((16, span), BF).at[:, :4].set(anc_y[None])
    update = share(jnp.concatenate([update, names], axis=0), "leaf", LEAF)
    slots = update[:, width, :4].reshape(-1).astype(jnp.int32)
    slots = lax.rem(slots - y * 16 + core * 8, 16)

    root_part = call(
        place_kernel,
        jax.ShapeDtypeStruct((Y, width, ZLO * QUARTER), BF),
        [pltpu.VMEM((width, 2 * rows), F32)],
        (update, side_own, side_oth, packed, packed_oth),
        (slots,),
        (root_block, root_block),
    )
    pairs = slots.reshape(LEAF, CORE, 2)
    pairs = jnp.where(core == 0, pairs, pairs[:, ::-1]).reshape(-1)
    sol = call(
        spread_kernel,
        jax.ShapeDtypeStruct((LEAF, 2 * width, span), BF),
        [pltpu.VMEM((width, 2 * rows), F32)],
        (exchange(root_part, "y"), packed, packed_oth),
        (pairs,),
        (root_block, root_block),
    )
    sol = total(exchange(sol, "leaf")).astype(BF)
    picked, root = share(sol[:width], "zhi", ZHI), sol[width:]

    cols = ZHI * ZLO
    root = jnp.transpose(root.reshape(CORE, 2, few, span), (0, 2, 1, 3)).reshape(CORE, few, rows)
    root = jnp.stack([jnp.where(core == 0, root[0], root[1]), jnp.where(core == 0, root[1], root[0])])
    root = jnp.transpose(root.reshape(CORE, few, cols, -1), (2, 0, 1, 3)).reshape(cols, -1)
    root, picked = lax.optimization_barrier((root, picked))

    correction = call(
        correct_kernel,
        jax.ShapeDtypeStruct((Y, width, ZLO * n), BF),
        [],
        (picked, packed, packed_oth),
        (),
        (panel_block, panel_block),
    )
    inv_own, correction = lax.optimization_barrier((inv_own, correction))
    inv_oth = lax.ppermute(inv_own, "core", other)
    child = call(
        solve_kernel,
        jax.ShapeDtypeStruct((CORE, lanes, width), BF),
        [],
        (forward_all, exchange(correction, "y"), inv_own, inv_oth),
        (jnp.array([core], jnp.int32),),
    )

    child = jnp.transpose(child.reshape(CORE, cols, -1, width), (1, 0, 2, 3)).reshape(cols, -1)
    n_child = child.shape[1]
    out = exchange(jnp.concatenate([child, root], axis=1).reshape(cols, -1, TILE), Z)
    out = total(out.reshape(ZHI, ZLO, -1)).astype(BF)
    child = jnp.transpose(out[:, :n_child].reshape(ZLO, CORE, -1), (1, 0, 2)).reshape(CORE, -1)
    root = jnp.transpose(out[:, n_child:].reshape(ZLO, CORE, -1), (1, 0, 2)).reshape(CORE, -1)
    n_child = child.shape[1]
    out = jnp.concatenate([child, root], axis=1)
    out = jnp.broadcast_to(out[None], (LEAF,) + out.shape).reshape(LEAF * CORE, -1, TILE)
    out = exchange(out, ("leaf", "core")).reshape(LEAF, CORE, -1)
    child = lax.dynamic_index_in_dim(out, leaf, 0, keepdims=False)[:, :n_child]
    child = jnp.transpose(child.reshape(CORE * ZLO, -1, width), (1, 0, 2)).reshape(-1, CORE * half)
    root = out[:, :, n_child:].reshape(LEAF, CORE, ZLO, few, -1)
    root = jnp.transpose(root, (4, 1, 2, 0, 3)).reshape(-1, CORE * half)
    return child[None], root


def solution(mesh):
    split = Mesh(
        mesh.devices.reshape(LEAF, Y, CORE, ZHI, ZLO), ("leaf", "y", "core", "zhi", "zlo")
    )
    row, col = ("y", "core"), ("zhi", "zlo")
    in_specs = (
        P("leaf", col, row),
        P("leaf", row, col),
        P("leaf", row, None),
        P("leaf", row),
        P(col, row),
        P(row, None),
    )
    out_specs = (P("leaf", row + col, None), P(row + col, None))
    return jax.shard_map(body, mesh=split, in_specs=in_specs, out_specs=out_specs, check_vma=False)
```

```python
import jax
import jax.numpy as jnp
from jax import lax
from jax.experimental import pallas as pl
from jax.experimental.pallas import tpu as pltpu
from jax.sharding import Mesh, PartitionSpec as P

BF = jnp.bfloat16
F32 = jnp.float32
TILE = 128
LEAF, Y, CORE, ZHI, ZLO = 4, 4, 2, 4, 8
Z = ("zhi", "zlo")


def exchange(x, axis):
    return lax.all_to_all(x, axis, 0, 0, tiled=True)


def share(x, axis, n):
    return exchange(jnp.broadcast_to(x[None], (n,) + x.shape), axis)


def total(parts):
    return jnp.sum(parts.astype(F32), axis=0)


def dot(a, b, contract):
    return lax.dot_general(a, b, (contract, ((), ())), preferred_element_type=F32)


QUARTER, INV = 64, 128
ROOT_ROWS, INV_ROWS, PANEL_ROWS = (0, 128), (128, 128), (256, 64)


def pack_kernel(leaf_ref, root_ref, inv_ref, panel_ref, out_ref):
    lanes = out_ref.shape[1]
    at = pl.ds(pl.multiple_of(leaf_ref[0] * QUARTER, QUARTER), QUARTER)
    out_ref[:QUARTER] = root_ref[at, :lanes]
    out_ref[QUARTER:2 * QUARTER] = root_ref[at, lanes:]
    out_ref[INV_ROWS[0]:PANEL_ROWS[0]] = inv_ref[...]
    fold = lanes // TILE
    few = panel_ref.shape[0] // fold
    for f in range(fold):
        out_ref[PANEL_ROWS[0]:, f * TILE:(f + 1) * TILE] = panel_ref[f * few:(f + 1) * few]


def fetch(refs, span, buf_ref, sems):
    copies = [
        pltpu.make_async_copy(ref.at[:, pl.ds(*span)], buf_ref.at[i], sems.at[i])
        for i, ref in enumerate(refs)
    ]
    for copy in copies:
        copy.start()
    return copies


def root_half(buf_ref, i):
    j = i % 2
    return buf_ref[i // 2, :, j * QUARTER:(j + 1) * QUARTER, :].reshape(ZLO * QUARTER, buf_ref.shape[3])


def place_kernel(slot_ref, upd_ref, rhs_own, rhs_oth, own_ref, oth_ref, out_ref, buf_ref, sems, side_ref):
    copies = fetch((own_ref, oth_ref), ROOT_ROWS, buf_ref, sems)
    half = rhs_own.shape[1]
    lanes = buf_ref.shape[3]
    side_ref[:, :half] = rhs_own[...].astype(F32)
    side_ref[:, half:] = rhs_oth[...].astype(F32)
    width = side_ref.shape[0]
    for k in range(LEAF):
        for u in range(4):
            at = pl.ds(pl.multiple_of(slot_ref[k * 4 + u] * TILE, TILE), TILE)
            side_ref[:, at] = side_ref[:, at] - upd_ref[k, :width, u * TILE:(u + 1) * TILE].astype(F32)
    for copy in copies:
        copy.wait()
    out = 0.0
    for i in range(4):
        side = side_ref[:, i * lanes:(i + 1) * lanes].astype(BF)
        out = out + dot(side, root_half(buf_ref, i), ((1,), (1,)))
    for k in range(Y):
        out_ref[k] = out.astype(BF)


def spread_kernel(slot_ref, parts_ref, own_ref, oth_ref, out_ref, buf_ref, sems, sol_ref):
    copies = fetch((own_ref, oth_ref), ROOT_ROWS, buf_ref, sems)
    lanes = buf_ref.shape[3]
    forward = parts_ref[0].astype(F32)
    for k in range(1, Y):
        forward = forward + parts_ref[k].astype(F32)
    forward = forward.astype(BF)
    for copy in copies:
        copy.wait()
    for i in range(4):
        sol_ref[:, i * lanes:(i + 1) * lanes] = dot(forward, root_half(buf_ref, i), ((1,), (0,)))
    width, span = forward.shape[0], 4 * TILE
    few = width // LEAF
    for k in range(LEAF):
        for u in range(4):
            at = pl.ds(pl.multiple_of(slot_ref[k * 4 + u] * TILE, TILE), TILE)
            out_ref[k, :width, u * TILE:(u + 1) * TILE] = sol_ref[:, at].astype(BF)
        mine = sol_ref[k * few:(k + 1) * few, :]
        mine = jnp.concatenate([mine[:, j * span:(j + 1) * span] for j in range(4)], axis=0)
        out_ref[k, width:, :] = mine.astype(BF)


def correct_kernel(parts_ref, own_ref, oth_ref, out_ref, buf_ref, sems):
    copies = fetch((own_ref, oth_ref), PANEL_ROWS, buf_ref, sems)
    picked = parts_ref[0].astype(F32)
    for k in range(1, ZHI):
        picked = picked + parts_ref[k].astype(F32)
    picked = picked.astype(BF)
    half = picked.shape[1] // 2
    n, lanes = TILE, buf_ref.shape[3]
    for copy in copies:
        copy.wait()
    for z in range(ZLO):
        out = 0.0
        for i in range(CORE):
            panel = jnp.concatenate([buf_ref[i, z, :, f:f + TILE] for f in range(0, lanes, TILE)], axis=0)
            out = out + dot(picked[:, i * half:(i + 1) * half], panel, ((1,), (0,)))
        for k in range(Y):
            out_ref[k, :, z * n:(z + 1) * n] = out.astype(BF)


def solve_kernel(core_ref, forward_ref, parts_ref, own_ref, oth_ref, out_ref, buf_ref, sems):
    copies = fetch((own_ref, oth_ref), INV_ROWS, buf_ref, sems)
    correction = parts_ref[0].astype(F32)
    for k in range(1, Y):
        correction = correction + parts_ref[k].astype(F32)
    residue = forward_ref[...].astype(F32) - correction.astype(BF).astype(F32)
    residue = residue.astype(BF)
    core = core_ref[0]
    for copy in copies:
        copy.wait()
    for i in range(CORE):
        inv = buf_ref[i].reshape(ZLO * INV, buf_ref.shape[3])
        out_ref[(core + i) % CORE] = dot(inv, residue, ((0,), (1,))).astype(BF)


def call(kernel, out_shape, inputs, scalars=(), gathered=(), span=None, scratch=()):
    vmem = pl.BlockSpec(memory_space=pltpu.VMEM)
    buffers = []
    if gathered:
        blocks, _, lanes = gathered[0].shape
        buffers = [pltpu.VMEM((len(gathered), blocks, span[1], lanes), BF), pltpu.SemaphoreType.DMA((len(gathered),))]
    return pl.pallas_call(
        kernel,
        out_shape=out_shape,
        in_specs=[pl.BlockSpec(memory_space=pltpu.SMEM)] * len(scalars)
        + [vmem] * len(inputs)
        + [pl.BlockSpec(memory_space=pl.ANY)] * len(gathered),
        out_specs=vmem,
        scratch_shapes=buffers + list(scratch),
    )(*scalars, *inputs, *gathered)


def body(child_inv, child_panel, child_rhs, anc_tiles, root_inv, root_rhs):
    inv, panel, rhs, anc = child_inv[0], child_panel[0], child_rhs[0], anc_tiles[0]
    y, core = lax.axis_index("y"), lax.axis_index("core")
    leaf, zlo = lax.axis_index("leaf"), lax.axis_index("zlo")
    rows = root_rhs.shape[0]
    other = [(0, 1), (1, 0)]
    half = rhs.shape[1] // CORE
    width = half // ZLO
    few = width // LEAF

    n = inv.shape[0]
    lanes = inv.shape[1]
    packed = call(
        pack_kernel,
        jax.ShapeDtypeStruct((sum(PANEL_ROWS), lanes), BF),
        (root_inv, inv, panel),
        (jnp.array([leaf], jnp.int32),),
    )
    packed = lax.all_gather(packed, "zlo", axis=0, tiled=False)

    part = dot(rhs, inv, ((0,), (1,))).astype(BF).reshape(CORE, half, n)
    chunk = lax.dynamic_slice_in_dim(
        root_rhs.reshape(rows, CORE, ZLO, width), zlo, 1, axis=2
    )[:, :, 0]
    chunk = jnp.transpose(chunk, (1, 2, 0)).reshape(CORE, width * rows // n, n)
    names = jnp.zeros((16, n), BF).at[:, :2].set(anc.astype(BF)[None])
    local_part = jnp.concatenate([panel, names], axis=0)
    local_part = jnp.broadcast_to(local_part[None], (CORE,) + local_part.shape)
    first = exchange(jnp.concatenate([part, chunk, local_part], axis=1), "core")
    at = [half, half + chunk.shape[1], half + chunk.shape[1] + panel.shape[0]]
    forward = total(share(total(first[:, :at[0]]).astype(BF), "y", Y)).astype(BF)
    side = first[:, at[0]:at[1]].reshape(CORE, width, rows)
    side_own = jnp.where(core == 0, side[0], side[1])
    side_oth = jnp.where(core == 0, side[1], side[0])
    panel_y = first[:, at[1]:at[2]].reshape(-1, n)
    anc_y = first[:, at[2], :2].reshape(-1)

    update = dot(forward, panel_y, ((1,), (1,))).astype(BF)
    span = update.shape[1]
    both = jnp.concatenate([update, forward], axis=1).reshape(ZLO, width, -1)
    both = exchange(both, "zlo")
    forward_all = jnp.transpose(both[:, :, span:], (1, 0, 2)).reshape(width, -1)
    update = total(both[:, :, :span]).astype(BF)
    update = total(share(update, "zhi", ZHI)).astype(BF)
    names = jnp.zeros((16, span), BF).at[:, :4].set(anc_y[None])
    update = share(jnp.concatenate([update, names], axis=0), "leaf", LEAF)
    packed, update = lax.optimization_barrier((packed, update))
    both = (packed, lax.ppermute(packed, "core", other))
    slots = update[:, width, :4].reshape(-1).astype(jnp.int32)
    slots = lax.rem(slots - y * 16 + core * 8, 16)

    wide = [pltpu.VMEM((width, 2 * rows), F32)]
    root_part = call(
        place_kernel,
        jax.ShapeDtypeStruct((Y, width, ZLO * QUARTER), BF),
        (update, side_own, side_oth),
        (slots,),
        both,
        ROOT_ROWS,
        wide,
    )
    pairs = slots.reshape(LEAF, CORE, 2)
    pairs = jnp.where(core == 0, pairs, pairs[:, ::-1]).reshape(-1)
    sol = call(
        spread_kernel,
        jax.ShapeDtypeStruct((LEAF, 2 * width, span), BF),
        (exchange(root_part, "y"),),
        (pairs,),
        both,
        ROOT_ROWS,
        wide,
    )
    sol = total(exchange(sol, "leaf")).astype(BF)
    picked, root = share(sol[:width], "zhi", ZHI), sol[width:]

    cols = ZHI * ZLO
    root = jnp.transpose(root.reshape(CORE, 2, few, span), (0, 2, 1, 3)).reshape(CORE, few, rows)
    root = jnp.stack([jnp.where(core == 0, root[0], root[1]), jnp.where(core == 0, root[1], root[0])])
    root = jnp.transpose(root.reshape(CORE, few, cols, -1), (2, 0, 1, 3)).reshape(cols, -1)
    root, picked = lax.optimization_barrier((root, picked))

    correction = call(
        correct_kernel,
        jax.ShapeDtypeStruct((Y, width, ZLO * n), BF),
        (picked,),
        (),
        both,
        PANEL_ROWS,
    )
    child = call(
        solve_kernel,
        jax.ShapeDtypeStruct((CORE, lanes, width), BF),
        (forward_all, exchange(correction, "y")),
        (jnp.array([core], jnp.int32),),
        both,
        INV_ROWS,
    )

    child = jnp.transpose(child.reshape(CORE, cols, -1, width), (1, 0, 2, 3)).reshape(cols, -1)
    n_child = child.shape[1]
    out = exchange(jnp.concatenate([child, root], axis=1).reshape(cols, -1, TILE), Z)
    out = total(out.reshape(ZHI, ZLO, -1)).astype(BF)
    child = jnp.transpose(out[:, :n_child].reshape(ZLO, CORE, -1), (1, 0, 2)).reshape(CORE, -1)
    root = jnp.transpose(out[:, n_child:].reshape(ZLO, CORE, -1), (1, 0, 2)).reshape(CORE, -1)
    n_child = child.shape[1]
    out = jnp.concatenate([child, root], axis=1)
    out = jnp.broadcast_to(out[None], (LEAF,) + out.shape).reshape(LEAF * CORE, -1, TILE)
    out = exchange(out, ("leaf", "core")).reshape(LEAF, CORE, -1)
    child = lax.dynamic_index_in_dim(out, leaf, 0, keepdims=False)[:, :n_child]
    child = jnp.transpose(child.reshape(CORE * ZLO, -1, width), (1, 0, 2)).reshape(-1, CORE * half)
    root = out[:, :, n_child:].reshape(LEAF, CORE, ZLO, few, -1)
    root = jnp.transpose(root, (4, 1, 2, 0, 3)).reshape(-1, CORE * half)
    return child[None], root


def solution(mesh):
    split = Mesh(
        mesh.devices.reshape(LEAF, Y, CORE, ZHI, ZLO), ("leaf", "y", "core", "zhi", "zlo")
    )
    row, col = ("y", "core"), ("zhi", "zlo")
    in_specs = (
        P("leaf", col, row),
        P("leaf", row, col),
        P("leaf", row, None),
        P("leaf", row),
        P(col, row),
        P(row, None),
    )
    out_specs = (P("leaf", row + col, None), P(row + col, None))
    return jax.shard_map(body, mesh=split, in_specs=in_specs, out_specs=out_specs, check_vma=False)
```

```python
import jax
import jax.numpy as jnp
from jax import lax
from jax.experimental import pallas as pl
from jax.experimental.pallas import tpu as pltpu
from jax.sharding import Mesh, PartitionSpec as P

BF = jnp.bfloat16
F32 = jnp.float32
TILE = 128
LEAF, Y, CORE, ZHI, ZLO = 4, 4, 2, 4, 8
Z = ("zhi", "zlo")


def exchange(x, axis):
    return lax.all_to_all(x, axis, 0, 0, tiled=True)


def share(x, axis, n):
    return exchange(jnp.broadcast_to(x[None], (n,) + x.shape), axis)


def total(parts):
    return jnp.sum(parts.astype(F32), axis=0)


def dot(a, b, contract):
    return lax.dot_general(a, b, (contract, ((), ())), preferred_element_type=F32)


QUARTER, INV = 64, 128
ROOT_ROWS, INV_ROWS, PANEL_ROWS = (0, 128), (128, 128), (256, 64)


def pack_kernel(leaf_ref, root_ref, inv_ref, panel_ref, out_ref):
    lanes = out_ref.shape[1]
    at = pl.ds(pl.multiple_of(leaf_ref[0] * QUARTER, QUARTER), QUARTER)
    out_ref[:QUARTER] = root_ref[at, :lanes]
    out_ref[QUARTER:2 * QUARTER] = root_ref[at, lanes:]
    out_ref[INV_ROWS[0]:PANEL_ROWS[0]] = inv_ref[...]
    fold = lanes // TILE
    few = panel_ref.shape[0] // fold
    for f in range(fold):
        out_ref[PANEL_ROWS[0]:, f * TILE:(f + 1) * TILE] = panel_ref[f * few:(f + 1) * few]


def root_half(refs, i):
    ref, j = refs[i // 2], i % 2
    return ref[:, j * QUARTER:(j + 1) * QUARTER, :].reshape(ZLO * QUARTER, ref.shape[2])


def place_kernel(slot_ref, upd_ref, rhs_own, rhs_oth, own_ref, oth_ref, out_ref, side_ref):
    half = rhs_own.shape[1]
    lanes = own_ref.shape[2]
    side_ref[:, :half] = rhs_own[...].astype(F32)
    side_ref[:, half:] = rhs_oth[...].astype(F32)
    width = side_ref.shape[0]
    for k in range(LEAF):
        for u in range(4):
            at = pl.ds(pl.multiple_of(slot_ref[k * 4 + u] * TILE, TILE), TILE)
            side_ref[:, at] = side_ref[:, at] - upd_ref[k, :width, u * TILE:(u + 1) * TILE].astype(F32)
    out = 0.0
    for i in range(4):
        side = side_ref[:, i * lanes:(i + 1) * lanes].astype(BF)
        out = out + dot(side, root_half((own_ref, oth_ref), i), ((1,), (1,)))
    for k in range(Y):
        out_ref[k] = out.astype(BF)


def spread_kernel(slot_ref, parts_ref, own_ref, oth_ref, out_ref, sol_ref):
    lanes = own_ref.shape[2]
    forward = parts_ref[0].astype(F32)
    for k in range(1, Y):
        forward = forward + parts_ref[k].astype(F32)
    forward = forward.astype(BF)
    for i in range(4):
        sol_ref[:, i * lanes:(i + 1) * lanes] = dot(forward, root_half((own_ref, oth_ref), i), ((1,), (0,)))
    width, span = forward.shape[0], 4 * TILE
    few = width // LEAF
    for k in range(LEAF):
        for u in range(4):
            at = pl.ds(pl.multiple_of(slot_ref[k * 4 + u] * TILE, TILE), TILE)
            out_ref[k, :width, u * TILE:(u + 1) * TILE] = sol_ref[:, at].astype(BF)
        mine = sol_ref[k * few:(k + 1) * few, :]
        mine = jnp.concatenate([mine[:, j * span:(j + 1) * span] for j in range(4)], axis=0)
        out_ref[k, width:, :] = mine.astype(BF)


def correct_kernel(parts_ref, own_ref, oth_ref, out_ref):
    picked = parts_ref[0].astype(F32)
    for k in range(1, ZHI):
        picked = picked + parts_ref[k].astype(F32)
    picked = picked.astype(BF)
    half = picked.shape[1] // 2
    n, lanes = TILE, own_ref.shape[2]
    for z in range(ZLO):
        out = 0.0
        for i, ref in enumerate((own_ref, oth_ref)):
            panel = jnp.concatenate([ref[z, :, f:f + TILE] for f in range(0, lanes, TILE)], axis=0)
            out = out + dot(picked[:, i * half:(i + 1) * half], panel, ((1,), (0,)))
        for k in range(Y):
            out_ref[k, :, z * n:(z + 1) * n] = out.astype(BF)


def solve_kernel(core_ref, forward_ref, parts_ref, own_ref, oth_ref, out_ref):
    correction = parts_ref[0].astype(F32)
    for k in range(1, Y):
        correction = correction + parts_ref[k].astype(F32)
    residue = forward_ref[...].astype(F32) - correction.astype(BF).astype(F32)
    residue = residue.astype(BF)
    core = core_ref[0]
    for i, ref in enumerate((own_ref, oth_ref)):
        inv = ref[...].reshape(ZLO * INV, ref.shape[2])
        out_ref[(core + i) % CORE] = dot(inv, residue, ((0,), (1,))).astype(BF)


def call(kernel, out_shape, inputs, scalars=(), gathered=(), span=None, scratch=()):
    vmem = pl.BlockSpec(memory_space=pltpu.VMEM)
    inputs = tuple(inputs) + tuple(g[:, span[0]:span[0] + span[1]] for g in gathered)
    return pl.pallas_call(
        kernel,
        out_shape=out_shape,
        in_specs=[pl.BlockSpec(memory_space=pltpu.SMEM)] * len(scalars) + [vmem] * len(inputs),
        out_specs=vmem,
        scratch_shapes=list(scratch),
        compiler_params=pltpu.CompilerParams(vmem_limit_bytes=16 * 1024 * 1024),
    )(*scalars, *inputs)


def body(child_inv, child_panel, child_rhs, anc_tiles, root_inv, root_rhs):
    inv, panel, rhs, anc = child_inv[0], child_panel[0], child_rhs[0], anc_tiles[0]
    y, core = lax.axis_index("y"), lax.axis_index("core")
    leaf, zlo = lax.axis_index("leaf"), lax.axis_index("zlo")
    rows = root_rhs.shape[0]
    other = [(0, 1), (1, 0)]
    half = rhs.shape[1] // CORE
    width = half // ZLO
    few = width // LEAF

    n = inv.shape[0]
    lanes = inv.shape[1]
    packed = call(
        pack_kernel,
        jax.ShapeDtypeStruct((sum(PANEL_ROWS), lanes), BF),
        (root_inv, inv, panel),
        (jnp.array([leaf], jnp.int32),),
    )
    packed = lax.all_gather(packed, "zlo", axis=0, tiled=False)

    part = dot(rhs, inv, ((0,), (1,))).astype(BF).reshape(CORE, half, n)
    chunk = lax.dynamic_slice_in_dim(
        root_rhs.reshape(rows, CORE, ZLO, width), zlo, 1, axis=2
    )[:, :, 0]
    chunk = jnp.transpose(chunk, (1, 2, 0)).reshape(CORE, width * rows // n, n)
    names = jnp.zeros((16, n), BF).at[:, :2].set(anc.astype(BF)[None])
    local_part = jnp.concatenate([panel, names], axis=0)
    local_part = jnp.broadcast_to(local_part[None], (CORE,) + local_part.shape)
    first = exchange(jnp.concatenate([part, chunk, local_part], axis=1), "core")
    at = [half, half + chunk.shape[1], half + chunk.shape[1] + panel.shape[0]]
    forward = total(share(total(first[:, :at[0]]).astype(BF), "y", Y)).astype(BF)
    side = first[:, at[0]:at[1]].reshape(CORE, width, rows)
    side_own = jnp.where(core == 0, side[0], side[1])
    side_oth = jnp.where(core == 0, side[1], side[0])
    panel_y = first[:, at[1]:at[2]].reshape(-1, n)
    anc_y = first[:, at[2], :2].reshape(-1)

    update = dot(forward, panel_y, ((1,), (1,))).astype(BF)
    span = update.shape[1]
    both = jnp.concatenate([update, forward], axis=1).reshape(ZLO, width, -1)
    both = exchange(both, "zlo")
    forward_all = jnp.transpose(both[:, :, span:], (1, 0, 2)).reshape(width, -1)
    update = total(both[:, :, :span]).astype(BF)
    update = total(share(update, "zhi", ZHI)).astype(BF)
    names = jnp.zeros((16, span), BF).at[:, :4].set(anc_y[None])
    update = share(jnp.concatenate([update, names], axis=0), "leaf", LEAF)
    packed, update = lax.optimization_barrier((packed, update))
    both = (packed, lax.ppermute(packed, "core", other))
    slots = update[:, width, :4].reshape(-1).astype(jnp.int32)
    slots = lax.rem(slots - y * 16 + core * 8, 16)

    wide = [pltpu.VMEM((width, 2 * rows), F32)]
    root_part = call(
        place_kernel,
        jax.ShapeDtypeStruct((Y, width, ZLO * QUARTER), BF),
        (update, side_own, side_oth),
        (slots,),
        both,
        ROOT_ROWS,
        wide,
    )
    pairs = slots.reshape(LEAF, CORE, 2)
    pairs = jnp.where(core == 0, pairs, pairs[:, ::-1]).reshape(-1)
    sol = call(
        spread_kernel,
        jax.ShapeDtypeStruct((LEAF, 2 * width, span), BF),
        (exchange(root_part, "y"),),
        (pairs,),
        both,
        ROOT_ROWS,
        wide,
    )
    sol = total(exchange(sol, "leaf")).astype(BF)
    picked, root = share(sol[:width], "zhi", ZHI), sol[width:]

    cols = ZHI * ZLO
    root = jnp.transpose(root.reshape(CORE, 2, few, span), (0, 2, 1, 3)).reshape(CORE, few, rows)
    root = jnp.stack([jnp.where(core == 0, root[0], root[1]), jnp.where(core == 0, root[1], root[0])])
    root = jnp.transpose(root.reshape(CORE, few, cols, -1), (2, 0, 1, 3)).reshape(cols, -1)
    root, picked = lax.optimization_barrier((root, picked))

    correction = call(
        correct_kernel,
        jax.ShapeDtypeStruct((Y, width, ZLO * n), BF),
        (picked,),
        (),
        both,
        PANEL_ROWS,
    )
    child = call(
        solve_kernel,
        jax.ShapeDtypeStruct((CORE, lanes, width), BF),
        (forward_all, exchange(correction, "y")),
        (jnp.array([core], jnp.int32),),
        both,
        INV_ROWS,
    )

    child = jnp.transpose(child.reshape(CORE, cols, -1, width), (1, 0, 2, 3)).reshape(cols, -1)
    n_child = child.shape[1]
    out = exchange(jnp.concatenate([child, root], axis=1).reshape(cols, -1, TILE), Z)
    out = total(out.reshape(ZHI, ZLO, -1)).astype(BF)
    child = jnp.transpose(out[:, :n_child].reshape(ZLO, CORE, -1), (1, 0, 2)).reshape(CORE, -1)
    root = jnp.transpose(out[:, n_child:].reshape(ZLO, CORE, -1), (1, 0, 2)).reshape(CORE, -1)
    n_child = child.shape[1]
    out = jnp.concatenate([child, root], axis=1)
    out = jnp.broadcast_to(out[None], (LEAF,) + out.shape).reshape(LEAF * CORE, -1, TILE)
    out = exchange(out, ("leaf", "core")).reshape(LEAF, CORE, -1)
    child = lax.dynamic_index_in_dim(out, leaf, 0, keepdims=False)[:, :n_child]
    child = jnp.transpose(child.reshape(CORE * ZLO, -1, width), (1, 0, 2)).reshape(-1, CORE * half)
    root = out[:, :, n_child:].reshape(LEAF, CORE, ZLO, few, -1)
    root = jnp.transpose(root, (4, 1, 2, 0, 3)).reshape(-1, CORE * half)
    return child[None], root


def solution(mesh):
    split = Mesh(
        mesh.devices.reshape(LEAF, Y, CORE, ZHI, ZLO), ("leaf", "y", "core", "zhi", "zlo")
    )
    row, col = ("y", "core"), ("zhi", "zlo")
    in_specs = (
        P("leaf", col, row),
        P("leaf", row, col),
        P("leaf", row, None),
        P("leaf", row),
        P(col, row),
        P(row, None),
    )
    out_specs = (P("leaf", row + col, None), P(row + col, None))
    return jax.shard_map(body, mesh=split, in_specs=in_specs, out_specs=out_specs, check_vma=False)
```

```python
import jax
import jax.numpy as jnp
from jax import lax
from jax.experimental import pallas as pl
from jax.experimental.pallas import tpu as pltpu
from jax.sharding import Mesh, PartitionSpec as P

BF = jnp.bfloat16
F32 = jnp.float32
TILE = 128
LEAF, Y, CORE, ZHI, ZLO = 4, 4, 2, 4, 8
Z = ("zhi", "zlo")


def exchange(x, axis):
    return lax.all_to_all(x, axis, 0, 0, tiled=True)


def share(x, axis, n):
    return exchange(jnp.broadcast_to(x[None], (n,) + x.shape), axis)


def total(parts):
    return jnp.sum(parts.astype(F32), axis=0)


def dot(a, b, contract):
    return lax.dot_general(a, b, (contract, ((), ())), preferred_element_type=F32)


QUARTER, INV = 64, 128
ROOT_ROWS, INV_ROWS, PANEL_ROWS = (0, 128), (128, 128), (256, 64)


def pack_kernel(leaf_ref, root_ref, inv_ref, panel_ref, out_ref):
    lanes = out_ref.shape[1]
    at = pl.ds(pl.multiple_of(leaf_ref[0] * QUARTER, QUARTER), QUARTER)
    out_ref[:QUARTER] = root_ref[at, :lanes]
    out_ref[QUARTER:2 * QUARTER] = root_ref[at, lanes:]
    out_ref[INV_ROWS[0]:PANEL_ROWS[0]] = inv_ref[...]
    fold = lanes // TILE
    few = panel_ref.shape[0] // fold
    for f in range(fold):
        out_ref[PANEL_ROWS[0]:, f * TILE:(f + 1) * TILE] = panel_ref[f * few:(f + 1) * few]


def root_half(refs, i):
    ref, j = refs[i // 2], i % 2
    return ref[:, j * QUARTER:(j + 1) * QUARTER, :].reshape(ZLO * QUARTER, ref.shape[2])


def place_kernel(slot_ref, upd_ref, rhs_own, rhs_oth, own_ref, oth_ref, out_ref, side_ref):
    half = rhs_own.shape[1]
    lanes = own_ref.shape[2]
    side_ref[:, :half] = rhs_own[...].astype(F32)
    side_ref[:, half:] = rhs_oth[...].astype(F32)
    width = side_ref.shape[0]
    for k in range(LEAF):
        for u in range(4):
            at = pl.ds(pl.multiple_of(slot_ref[k * 4 + u] * TILE, TILE), TILE)
            side_ref[:, at] = side_ref[:, at] - upd_ref[k, :width, u * TILE:(u + 1) * TILE].astype(F32)
    out = 0.0
    for i in range(4):
        side = side_ref[:, i * lanes:(i + 1) * lanes].astype(BF)
        out = out + dot(side, root_half((own_ref, oth_ref), i), ((1,), (1,)))
    for k in range(Y):
        out_ref[k] = out.astype(BF)


def spread_kernel(slot_ref, parts_ref, own_ref, oth_ref, out_ref, sol_ref):
    lanes = own_ref.shape[2]
    forward = parts_ref[0].astype(F32)
    for k in range(1, Y):
        forward = forward + parts_ref[k].astype(F32)
    forward = forward.astype(BF)
    for i in range(4):
        sol_ref[:, i * lanes:(i + 1) * lanes] = dot(forward, root_half((own_ref, oth_ref), i), ((1,), (0,)))
    width, span = forward.shape[0], 4 * TILE
    few = width // LEAF
    for k in range(LEAF):
        for u in range(4):
            at = pl.ds(pl.multiple_of(slot_ref[k * 4 + u] * TILE, TILE), TILE)
            out_ref[k, :width, u * TILE:(u + 1) * TILE] = sol_ref[:, at].astype(BF)
        mine = sol_ref[k * few:(k + 1) * few, :]
        mine = jnp.concatenate([mine[:, j * span:(j + 1) * span] for j in range(4)], axis=0)
        out_ref[k, width:, :] = mine.astype(BF)


def correct_kernel(parts_ref, own_ref, oth_ref, out_ref):
    picked = parts_ref[0].astype(F32)
    for k in range(1, ZHI):
        picked = picked + parts_ref[k].astype(F32)
    picked = picked.astype(BF)
    half = picked.shape[1] // 2
    n, lanes = TILE, own_ref.shape[2]
    for z in range(ZLO):
        out = 0.0
        for i, ref in enumerate((own_ref, oth_ref)):
            panel = jnp.concatenate([ref[z, :, f:f + TILE] for f in range(0, lanes, TILE)], axis=0)
            out = out + dot(picked[:, i * half:(i + 1) * half], panel, ((1,), (0,)))
        for k in range(Y):
            out_ref[k, :, z * n:(z + 1) * n] = out.astype(BF)


def solve_kernel(core_ref, forward_ref, parts_ref, own_ref, oth_ref, out_ref):
    correction = parts_ref[0].astype(F32)
    for k in range(1, Y):
        correction = correction + parts_ref[k].astype(F32)
    residue = forward_ref[...].astype(F32) - correction.astype(BF).astype(F32)
    residue = residue.astype(BF)
    core = core_ref[0]
    for i, ref in enumerate((own_ref, oth_ref)):
        inv = ref[...].reshape(ZLO * INV, ref.shape[2])
        out_ref[(core + i) % CORE] = dot(inv, residue, ((0,), (1,))).astype(BF)


def call(kernel, out_shape, inputs, scalars=(), gathered=(), span=None, scratch=()):
    vmem = pl.BlockSpec(memory_space=pltpu.VMEM)
    inputs = tuple(inputs) + tuple(g[:, span[0]:span[0] + span[1]] for g in gathered)
    return pl.pallas_call(
        kernel,
        out_shape=out_shape,
        in_specs=[pl.BlockSpec(memory_space=pltpu.SMEM)] * len(scalars) + [vmem] * len(inputs),
        out_specs=vmem,
        scratch_shapes=list(scratch),
        compiler_params=pltpu.CompilerParams(vmem_limit_bytes=16 * 1024 * 1024),
    )(*scalars, *inputs)


def body(child_inv, child_panel, child_rhs, anc_tiles, root_inv, root_rhs):
    inv, panel, rhs, anc = child_inv[0], child_panel[0], child_rhs[0], anc_tiles[0]
    y, core = lax.axis_index("y"), lax.axis_index("core")
    leaf, zlo = lax.axis_index("leaf"), lax.axis_index("zlo")
    rows = root_rhs.shape[0]
    other = [(0, 1), (1, 0)]
    half = rhs.shape[1] // CORE
    width = half // ZLO
    few = width // LEAF

    n = inv.shape[0]
    lanes = inv.shape[1]
    packed = call(
        pack_kernel,
        jax.ShapeDtypeStruct((sum(PANEL_ROWS), lanes), BF),
        (root_inv, inv, panel),
        (jnp.array([leaf], jnp.int32),),
    )
    packed = lax.all_gather(packed, "zlo", axis=0, tiled=False)

    part = dot(rhs, inv, ((0,), (1,))).astype(BF).reshape(CORE, half, n)
    chunk = lax.dynamic_slice_in_dim(
        root_rhs.reshape(rows, CORE, ZLO, width), zlo, 1, axis=2
    )[:, :, 0]
    chunk = jnp.transpose(chunk, (1, 2, 0)).reshape(CORE, width * rows // n, n)
    names = jnp.zeros((16, n), BF).at[:, :2].set(anc.astype(BF)[None])
    local_part = jnp.concatenate([panel, names], axis=0)
    local_part = jnp.broadcast_to(local_part[None], (CORE,) + local_part.shape)
    first = exchange(jnp.concatenate([part, chunk, local_part], axis=1), "core")
    at = [half, half + chunk.shape[1], half + chunk.shape[1] + panel.shape[0]]
    forward = total(share(total(first[:, :at[0]]).astype(BF), "y", Y)).astype(BF)
    side = first[:, at[0]:at[1]].reshape(CORE, width, rows)
    side_own = jnp.where(core == 0, side[0], side[1])
    side_oth = jnp.where(core == 0, side[1], side[0])
    panel_y = first[:, at[1]:at[2]].reshape(-1, n)
    anc_y = first[:, at[2], :2].reshape(-1)

    update = dot(forward, panel_y, ((1,), (1,))).astype(BF)
    span = update.shape[1]
    both = jnp.concatenate([update, forward], axis=1).reshape(ZLO, width, -1)
    both = exchange(both, "zlo")
    forward_all = jnp.transpose(both[:, :, span:], (1, 0, 2)).reshape(width, -1)
    update = total(both[:, :, :span]).astype(BF)
    update = total(share(update, "zhi", ZHI)).astype(BF)
    names = jnp.zeros((16, span), BF).at[:, :4].set(anc_y[None])
    update = share(jnp.concatenate([update, names], axis=0), "leaf", LEAF)
    packed, update = lax.optimization_barrier((packed, update))
    both = (packed, lax.ppermute(packed, "core", other))
    slots = update[:, width, :4].reshape(-1).astype(jnp.int32)
    slots = lax.rem(slots - y * 16 + core * 8, 16)

    wide = [pltpu.VMEM((width, 2 * rows), F32)]
    root_part = call(
        place_kernel,
        jax.ShapeDtypeStruct((Y, width, ZLO * QUARTER), BF),
        (update, side_own, side_oth),
        (slots,),
        both,
        ROOT_ROWS,
        wide,
    )
    pairs = slots.reshape(LEAF, CORE, 2)
    pairs = jnp.where(core == 0, pairs, pairs[:, ::-1]).reshape(-1)
    sol = call(
        spread_kernel,
        jax.ShapeDtypeStruct((LEAF, 2 * width, span), BF),
        (exchange(root_part, "y"),),
        (pairs,),
        both,
        ROOT_ROWS,
        wide,
    )
    sol = total(exchange(sol, "leaf")).astype(BF)
    both, sol = lax.optimization_barrier((both, sol))
    picked, root = share(sol[:width], "zhi", ZHI), sol[width:]

    cols = ZHI * ZLO
    root = jnp.transpose(root.reshape(CORE, 2, few, span), (0, 2, 1, 3)).reshape(CORE, few, rows)
    root = jnp.stack([jnp.where(core == 0, root[0], root[1]), jnp.where(core == 0, root[1], root[0])])
    root = jnp.transpose(root.reshape(CORE, few, cols, -1), (2, 0, 1, 3)).reshape(cols, -1)
    root, picked = lax.optimization_barrier((root, picked))

    correction = call(
        correct_kernel,
        jax.ShapeDtypeStruct((Y, width, ZLO * n), BF),
        (picked,),
        (),
        both,
        PANEL_ROWS,
    )
    child = call(
        solve_kernel,
        jax.ShapeDtypeStruct((CORE, lanes, width), BF),
        (forward_all, exchange(correction, "y")),
        (jnp.array([core], jnp.int32),),
        both,
        INV_ROWS,
    )

    child = jnp.transpose(child.reshape(CORE, cols, -1, width), (1, 0, 2, 3)).reshape(cols, -1)
    n_child = child.shape[1]
    out = exchange(jnp.concatenate([child, root], axis=1).reshape(cols, -1, TILE), Z)
    out = total(out.reshape(ZHI, ZLO, -1)).astype(BF)
    child = jnp.transpose(out[:, :n_child].reshape(ZLO, CORE, -1), (1, 0, 2)).reshape(CORE, -1)
    root = jnp.transpose(out[:, n_child:].reshape(ZLO, CORE, -1), (1, 0, 2)).reshape(CORE, -1)
    n_child = child.shape[1]
    out = jnp.concatenate([child, root], axis=1)
    out = jnp.broadcast_to(out[None], (LEAF,) + out.shape).reshape(LEAF * CORE, -1, TILE)
    out = exchange(out, ("leaf", "core")).reshape(LEAF, CORE, -1)
    child = lax.dynamic_index_in_dim(out, leaf, 0, keepdims=False)[:, :n_child]
    child = jnp.transpose(child.reshape(CORE * ZLO, -1, width), (1, 0, 2)).reshape(-1, CORE * half)
    root = out[:, :, n_child:].reshape(LEAF, CORE, ZLO, few, -1)
    root = jnp.transpose(root, (4, 1, 2, 0, 3)).reshape(-1, CORE * half)
    return child[None], root


def solution(mesh):
    split = Mesh(
        mesh.devices.reshape(LEAF, Y, CORE, ZHI, ZLO), ("leaf", "y", "core", "zhi", "zlo")
    )
    row, col = ("y", "core"), ("zhi", "zlo")
    in_specs = (
        P("leaf", col, row),
        P("leaf", row, col),
        P("leaf", row, None),
        P("leaf", row),
        P(col, row),
        P(row, None),
    )
    out_specs = (P("leaf", row + col, None), P(row + col, None))
    return jax.shard_map(body, mesh=split, in_specs=in_specs, out_specs=out_specs, check_vma=False)
```
